32 devices in a mesh: rep: 16 (over z, y, core), voc: 2 (over x).
Axes of the slice: x: 2, y: 2, z: 4, core: 2. Of those that a mesh axis runs over, the one named last changes fastest.
Arguments:
- states: bfloat16 [2, 256, 6144], P(None, None, 'rep'), may hold values from -6 to 6
- head_weight: bfloat16 [6144, 4096], P('rep', 'voc'), may hold values from -0.21875 to 0.21875
- pair_order: int32 [2, 8], replicated, may hold values from 0 to 7, each once within a row
- row_example: int32 [2, 8, 256], replicated, may hold values from 0 to 255, each once within a row
Outputs:
- state_grad: bfloat16 [2, 256, 6144], P(None, None, 'rep')
- head_grad: bfloat16 [6144, 4096], P('rep', 'voc')
The draws below stay inside these ranges and needn't reach their ends.
Inputs may be any that keep to these rules, and one draw needn't show every extreme that they name: Each row pair_order[m] holds every replica once. Each row row_example[m, r] holds every number of 0 to 255 once.
All inputs are finite; a program needn't handle non-finite values.
Results may differ from the reference program's by a relative error of at most 0.0055.
Values may be sent and summed in bfloat16 or wider, within the bound.
No kernel may reach another device: no remote copies, remote signals or barrier semaphores. Data moves between devices by JAX's collectives and lax.ppermute only.
A program may use at most 64 MiB of HBM per device.

```python
import jax
import jax.numpy as jnp
from jax import lax

D = 768
MB = 2
B = 256
REPLICAS = 8
V = 4096


def levels(stream_key, dims, pieces, low, largest):
    loudness = 1.0
    for dim, parts in pieces:
        steps = jax.random.uniform(jax.random.fold_in(jax.random.fold_in(stream_key, 6), dim), (parts,), jnp.float32, low / len(pieces), largest / len(pieces))
        loudness = loudness * jnp.repeat(jnp.exp(steps), dims[dim] // parts).reshape((-1,) + (1,) * (len(dims) - 1 - dim))
    return loudness


def scatter_about(rng, dims, deviation, limit, shards=(), kind=jnp.bfloat16):
    result = jax.random.normal(rng, dims, jnp.float32) * deviation
    if len(shards) > 0:
        result = levels(rng, dims, shards, -0.22, 0.18) * result
    return jnp.clip(result, min=-limit, max=limit).astype(kind)


def setup_inputs(seed: int = 0) -> dict:
    keys = jax.random.split(jax.random.key(seed), 5)
    states = scatter_about(keys[0], (MB, B, REPLICAS * D), 1.0, 6.0, ((2, 16),))
    head_weight = scatter_about(keys[1], (REPLICAS * D, V), D ** -0.5, 0.21875, ((0, 16), (1, 2)))
    pair_order = jax.vmap(lambda own: jax.random.permutation(own, REPLICAS))(jax.random.split(keys[2], MB)).reshape((MB, REPLICAS)).astype(jnp.int32)
    row_example = jax.vmap(lambda own: jax.random.permutation(own, B))(jax.random.split(keys[3], MB * REPLICAS)).reshape((MB, REPLICAS, B)).astype(jnp.int32)
    return {"states": states, "head_weight": head_weight, "pair_order": pair_order, "row_example": row_example}


distill_weight = 0.0625


def partner_table(pair_order):
    slot_count = pair_order.shape[1]
    slot_ids = jnp.arange(slot_count, dtype=jnp.int32)
    matches = pair_order[:, None, :] == slot_ids[None, :, None]
    position = jnp.sum(jnp.where(matches, slot_ids[None, None, :], 0), axis=2).astype(jnp.int32)
    following = ((position + 1) % slot_count).astype(jnp.int32)
    return jnp.take_along_axis(pair_order, following, axis=1)


def to_examples(rows_in, examples):
    slot_count = examples.shape[1]
    slot_ids = jnp.arange(slot_count, dtype=jnp.int32)
    onehot = (examples[:, None, :] == slot_ids[None, :, None]).astype(jnp.float32)
    return jnp.einsum("mei,miw->mew", onehot, rows_in.astype(jnp.float32)).astype(jnp.bfloat16)


def reference(states, head_weight, pair_order, row_example):
    micro_count, row_count, total_width = states.shape
    replica_count = pair_order.shape[1]
    width = total_width // replica_count
    vocab = head_weight.shape[1]
    partner = partner_table(pair_order)
    micro_ids = jnp.arange(micro_count, dtype=jnp.int32)

    def pieces_of(replica):
        block = lax.dynamic_slice_in_dim(states, replica * width, width, 2)
        weights = lax.dynamic_slice_in_dim(head_weight, replica * width, width, 0)
        examples = lax.dynamic_index_in_dim(row_example, replica, 1, keepdims=False)
        return to_examples(block, examples), weights, examples

    def logits_of(replica):
        ordered, weights, examples = pieces_of(replica)
        flat = jnp.dot(ordered.reshape(-1, width), weights, preferred_element_type=jnp.float32)
        return flat.astype(jnp.bfloat16).reshape(micro_count, row_count, vocab)

    replica_ids = jnp.arange(replica_count, dtype=jnp.int32)
    logits = lax.map(logits_of, replica_ids)

    def grads_of(replica):
        ordered, weights, examples = pieces_of(replica)
        own_logits = logits[replica]
        mates = partner[:, replica]
        mate_logits = logits[mates, micro_ids]
        gradient = (distill_weight * (own_logits.astype(jnp.float32) - mate_logits.astype(jnp.float32))).astype(jnp.bfloat16)
        flat_grad = gradient.reshape(-1, vocab)
        head_part = jnp.dot(ordered.reshape(-1, width).T, flat_grad, preferred_element_type=jnp.float32).astype(jnp.bfloat16)
        example_grad = jnp.dot(flat_grad, weights.T, preferred_element_type=jnp.float32).astype(jnp.bfloat16)
        example_grad = example_grad.reshape(micro_count, row_count, width)
        state_part = jnp.take_along_axis(example_grad, examples[:, :, None], axis=1)
        return state_part, head_part

    state_parts, head_parts = lax.map(grads_of, replica_ids)
    state_grad = state_parts.transpose(1, 2, 0, 3).reshape(micro_count, row_count, replica_count * width)
    head_grad = head_parts.reshape(replica_count * width, vocab)
    return state_grad, head_grad
```

```python
import functools
import itertools
import math

import jax
import jax.numpy as jnp
from jax import lax
from jax.experimental import pallas as pl
from jax.experimental.pallas import tpu as pltpu
from jax.sharding import PartitionSpec as P

distill_weight = 0.0625
max_branches = 24


def partner_table(pair_order):
    slot_count = pair_order.shape[1]
    slot_ids = jnp.arange(slot_count, dtype=jnp.int32)
    matches = pair_order[:, None, :] == slot_ids[None, :, None]
    following = jnp.roll(pair_order, -1, axis=1)
    return jnp.sum(jnp.where(matches, following[:, None, :], 0), axis=2)


def route_kernel(order_ref, branch_ref, parity_ref, dest, src, color):
    micro_count, replicas = order_ref.shape
    pairs = replicas // 2
    for m in range(micro_count):
        for k in range(replicas):
            to, frm = order_ref[m, k], order_ref[m, (k + 1) % replicas]
            dest[frm] = to
            src[to] = frm
            color[k] = -1
        for start in range(0, replicas, 2):
            at = jnp.where(color[start] == 1, start + 1, start)
            for _ in range(pairs):
                color[at] = 0
                color[at ^ 1] = 1
                at = src[dest[at ^ 1] ^ 1]
        for z in range(pairs):
            parity_ref[m, 0, z] = color[2 * z]
            parity_ref[m, 1, z] = color[src[2 * z]]
        for c in range(2):
            sigma = []
            place = jnp.int32(0)
            for z in range(pairs):
                leaves = jnp.where(color[2 * z] == c, 2 * z, 2 * z + 1)
                to = dest[leaves] // 2
                smaller = to
                for earlier in sigma:
                    smaller = smaller - jnp.where(earlier < to, 1, 0)
                place = place * (pairs - z) + smaller
                sigma.append(to)
            branch_ref[m, c] = place


def routes(pair_order):
    micro_count, replicas = pair_order.shape
    smem = pl.BlockSpec(memory_space=pltpu.SMEM)
    return pl.pallas_call(
        route_kernel,
        out_shape=(
            jax.ShapeDtypeStruct((micro_count, 2), jnp.int32),
            jax.ShapeDtypeStruct((micro_count, 2, replicas // 2), jnp.int32),
        ),
        in_specs=[smem],
        out_specs=(smem, smem),
        scratch_shapes=[pltpu.SMEM((replicas,), jnp.int32)] * 3,
    )(pair_order)


def move_pairs(block, branch, pairs):
    def one(sigma, moved):
        if all(z == to for z, to in enumerate(sigma)):
            return moved
        route = [(z * 4 + low, to * 4 + low) for z, to in enumerate(sigma) for low in range(4)]
        return lax.ppermute(moved, "rep", route)

    every = [functools.partial(one, sigma) for sigma in itertools.permutations(range(pairs))]
    return lax.switch(branch, every, block)


def swap(block, axis, bit):
    count = lax.axis_size(axis)
    return lax.ppermute(block, axis, [(i, i ^ bit) for i in range(count)])


def difference(own, other):
    spread = own.astype(jnp.float32) - other.astype(jnp.float32)
    return (distill_weight * spread).astype(jnp.bfloat16)


def sum_over(block, axis):
    if lax.axis_size(axis) == 2:
        return block + swap(block, axis, 1)
    return lax.psum(block, axis)


def paired_body(states, head_weight, pair_order, row_example):
    micro_count, row_count, half_width = states.shape
    place = lax.axis_index("rep")
    replica, side = place // 2, place % 2
    pair, parity = replica // 2, replica % 2
    pairs = pair_order.shape[1] // 2
    quarter = row_count // 4
    local = jnp.arange(row_count, dtype=jnp.int32)
    block = local // quarter
    example_of = (
        (side ^ (block & 1)) * (2 * quarter) + (parity ^ (block >> 1)) * quarter + local % quarter
    )
    examples = lax.dynamic_index_in_dim(row_example, replica, 1, keepdims=False)
    onehot = (examples[:, None, :] == example_of[None, :, None]).astype(jnp.bfloat16)
    branch, sides = routes(pair_order)
    mine = lax.dynamic_index_in_dim(sides, pair, 2, keepdims=False)

    ordered, homes, sibs = [], [], []
    for m in range(micro_count):
        rows = jnp.dot(onehot[m], states[m], preferred_element_type=jnp.float32)
        ordered.append(rows.astype(jnp.bfloat16))
        partial = jnp.dot(ordered[m], head_weight, preferred_element_type=jnp.float32)
        partial = partial.reshape(2, 2, quarter, -1)
        logits = (partial[:, 0] + swap(partial[:, 1], "rep", 1)).astype(jnp.bfloat16)
        homes.append(logits[0])
        sibs.append(swap(logits[1], "rep", 2))

    head_parts, state_parts = [], []
    for m in range(micro_count):
        home, sib = homes[m], sibs[m]
        home_first = mine[m, 0] == parity
        first = move_pairs(jnp.where(home_first, home, sib), branch[m, 0], pairs)
        second = move_pairs(jnp.where(home_first, sib, home), branch[m, 1], pairs)
        to_home_first = mine[m, 1] == parity
        grad_home = difference(home, jnp.where(to_home_first, first, second))
        grad_sib = difference(sib, jnp.where(to_home_first, second, first))
        near = jnp.concatenate([grad_home, swap(grad_home, "rep", 1)], axis=0)
        grad_far = swap(grad_sib, "rep", 2)
        far = jnp.concatenate([grad_far, swap(grad_far, "rep", 1)], axis=0)
        states_here = []
        for part, gradient in enumerate((near, far)):
            rows = ordered[m][part * 2 * quarter : (part + 1) * 2 * quarter]
            head_parts.append((rows, gradient))
            back = jnp.einsum(
                "rv,wv->rw", gradient, head_weight, preferred_element_type=jnp.float32
            )
            states_here.append(sum_over(back, "voc").astype(jnp.bfloat16))
        state_canon = jnp.concatenate(states_here, axis=0)
        state_parts.append(
            jnp.einsum("ei,ew->iw", onehot[m], state_canon, preferred_element_type=jnp.float32)
        )
    state_grad = jnp.stack(state_parts).astype(jnp.bfloat16)
    rows = jnp.concatenate([r for r, _ in head_parts], axis=0)
    gradient = jnp.concatenate([g for _, g in head_parts], axis=0)
    head_grad = jnp.einsum("rw,rv->wv", rows, gradient, preferred_element_type=jnp.float32)
    return state_grad, head_grad.astype(jnp.bfloat16)


def spread_body(states, head_weight, pair_order, row_example):
    micro_count, row_count, half_width = states.shape
    devices = lax.axis_size("rep")
    place = lax.axis_index("rep")
    replica, side = place // 2, place % 2
    half = row_count // 2
    local = jnp.arange(row_count, dtype=jnp.int32)
    example_of = (side ^ (local // half)) * half + local % half
    examples = lax.dynamic_index_in_dim(row_example, replica, 1, keepdims=False)
    onehot = (examples[:, None, :] == example_of[None, :, None]).astype(jnp.bfloat16)
    ordered = jnp.einsum("mei,miw->mew", onehot, states, preferred_element_type=jnp.float32)
    ordered = ordered.astype(jnp.bfloat16)
    partner = partner_table(pair_order)
    sources = jnp.arange(devices, dtype=jnp.int32)
    partner_dev = 2 * jnp.repeat(partner, 2, axis=1) + sources % 2
    state_parts, gradients = [], []
    for m in range(micro_count):
        partial = jnp.dot(ordered[m], head_weight, preferred_element_type=jnp.float32)
        logits = (partial[:half] + swap(partial[half:], "rep", 1)).astype(jnp.bfloat16)
        tiles = logits.reshape(devices, half // devices, -1)
        tiles = lax.all_to_all(tiles, "rep", split_axis=0, concat_axis=0, tiled=True)
        mates = (partner_dev[m][:, None] == sources[None, :]).astype(jnp.bfloat16)
        mate_tiles = jnp.einsum("ds,srv->drv", mates, tiles, preferred_element_type=jnp.float32)
        graded = difference(tiles, mate_tiles)
        graded = lax.all_to_all(graded, "rep", split_axis=0, concat_axis=0, tiled=True)
        graded = graded.reshape(half, -1)
        gradient = jnp.concatenate([graded, swap(graded, "rep", 1)], axis=0)
        gradients.append(gradient)
        back = jnp.einsum("rv,wv->rw", gradient, head_weight, preferred_element_type=jnp.float32)
        state_canon = sum_over(back, "voc").astype(jnp.bfloat16)
        state_parts.append(
            jnp.einsum("ei,ew->iw", onehot[m], state_canon, preferred_element_type=jnp.float32)
        )
    state_grad = jnp.stack(state_parts).astype(jnp.bfloat16)
    head_grad = jnp.einsum(
        "mrw,mrv->wv", ordered, jnp.stack(gradients), preferred_element_type=jnp.float32
    )
    return state_grad, head_grad.astype(jnp.bfloat16)


def solution(mesh):
    replicas = mesh.shape["rep"] // 2
    few = replicas % 2 == 0 and math.factorial(replicas // 2) <= max_branches
    return jax.shard_map(
        paired_body if few else spread_body,
        mesh=mesh,
        in_specs=(P(None, None, "rep"), P("rep", "voc"), P(), P()),
        out_specs=(P(None, None, "rep"), P("rep", "voc")),
        check_vma=False,
    )
```

```python
import functools
import itertools
import math

import jax
import jax.numpy as jnp
from jax import lax
from jax.experimental import pallas as pl
from jax.experimental.pallas import tpu as pltpu
from jax.sharding import PartitionSpec as P

distill_weight = 0.0625
max_branches = 24


def partner_table(pair_order):
    slot_count = pair_order.shape[1]
    slot_ids = jnp.arange(slot_count, dtype=jnp.int32)
    matches = pair_order[:, None, :] == slot_ids[None, :, None]
    following = jnp.roll(pair_order, -1, axis=1)
    return jnp.sum(jnp.where(matches, following[:, None, :], 0), axis=2)


def route_kernel(order_ref, branch_ref, parity_ref, dest, src, color):
    micro_count, replicas = order_ref.shape
    pairs = replicas // 2
    for m in range(micro_count):
        for k in range(replicas):
            to, frm = order_ref[m, k], order_ref[m, (k + 1) % replicas]
            dest[frm] = to
            src[to] = frm
            color[k] = -1
        for start in range(0, replicas, 2):
            at = jnp.where(color[start] == 1, start + 1, start)
            for _ in range(pairs):
                color[at] = 0
                color[at ^ 1] = 1
                at = src[dest[at ^ 1] ^ 1]
        for z in range(pairs):
            parity_ref[m, 0, z] = color[2 * z]
            parity_ref[m, 1, z] = color[src[2 * z]]
        for c in range(2):
            sigma = []
            place = jnp.int32(0)
            for z in range(pairs):
                leaves = jnp.where(color[2 * z] == c, 2 * z, 2 * z + 1)
                to = dest[leaves] // 2
                smaller = to
                for earlier in sigma:
                    smaller = smaller - jnp.where(earlier < to, 1, 0)
                place = place * (pairs - z) + smaller
                sigma.append(to)
            branch_ref[m, c] = place


def routes(pair_order):
    micro_count, replicas = pair_order.shape
    smem = pl.BlockSpec(memory_space=pltpu.SMEM)
    return pl.pallas_call(
        route_kernel,
        out_shape=(
            jax.ShapeDtypeStruct((micro_count, 2), jnp.int32),
            jax.ShapeDtypeStruct((micro_count, 2, replicas // 2), jnp.int32),
        ),
        in_specs=[smem],
        out_specs=(smem, smem),
        scratch_shapes=[pltpu.SMEM((replicas,), jnp.int32)] * 3,
    )(pair_order)


def move_pairs(block, branch, pairs):
    def one(sigma, moved):
        if all(z == to for z, to in enumerate(sigma)):
            return moved
        route = [(z * 4 + low, to * 4 + low) for z, to in enumerate(sigma) for low in range(4)]
        return lax.ppermute(moved, "rep", route)

    every = [functools.partial(one, sigma) for sigma in itertools.permutations(range(pairs))]
    return lax.switch(branch, every, block)


def swap(block, axis, bit):
    count = lax.axis_size(axis)
    return lax.ppermute(block, axis, [(i, i ^ bit) for i in range(count)])


def difference(own, other):
    spread = own.astype(jnp.float32) - other.astype(jnp.float32)
    return (distill_weight * spread).astype(jnp.bfloat16)


def sum_over(block, axis):
    if lax.axis_size(axis) == 2:
        return block + swap(block, axis, 1)
    return lax.psum(block, axis)


def after(block, *others):
    return lax.optimization_barrier((block, *others))[0]


def paired_body(states, head_weight, pair_order, row_example):
    micro_count, row_count, half_width = states.shape
    place = lax.axis_index("rep")
    replica, side = place // 2, place % 2
    pair, parity = replica // 2, replica % 2
    pairs = pair_order.shape[1] // 2
    quarter = row_count // 4
    local = jnp.arange(row_count, dtype=jnp.int32)
    block = local // quarter
    example_of = (
        (side ^ (block >> 1)) * (2 * quarter) + (parity ^ (block & 1)) * quarter + local % quarter
    )
    examples = lax.dynamic_index_in_dim(row_example, replica, 1, keepdims=False)
    onehot = (examples[:, None, :] == example_of[None, :, None]).astype(jnp.bfloat16)

    ordered, homes, fars = [], [], []
    for m in range(micro_count):
        rows = jnp.dot(onehot[m], states[m], preferred_element_type=jnp.float32)
        rows = rows.astype(jnp.bfloat16)
        ordered.append(rows)
        theirs = jnp.dot(rows[2 * quarter :], head_weight, preferred_element_type=jnp.float32)
        arrived = swap(theirs, "rep", 1)
        own = jnp.dot(rows[: 2 * quarter], head_weight, preferred_element_type=jnp.float32)
        fars.append((own[quarter:] + arrived[quarter:]).astype(jnp.bfloat16))
        homes.append((own[:quarter] + arrived[:quarter]).astype(jnp.bfloat16))
    sibs = []
    for m in range(micro_count):
        sibs.append(swap(after(fars[m], *sibs), "rep", 2))
    branch, sides = routes(after(pair_order, homes[0], fars[0]))
    mine = lax.dynamic_index_in_dim(sides, pair, 2, keepdims=False)

    grads_home, grads_sib, grads_far, nears, farthers = [], [], [], [], []
    for m in range(micro_count):
        home, sib = homes[m], sibs[m]
        home_first = mine[m, 0] == parity
        sent_first = jnp.where(home_first, home, sib)
        sent_second = jnp.where(home_first, sib, home)
        if m > 0:
            sent_first = after(sent_first, grads_home[-1], grads_sib[-1])
        first = move_pairs(sent_first, branch[m, 0], pairs)
        second = move_pairs(after(sent_second, first), branch[m, 1], pairs)
        to_home_first = mine[m, 1] == parity
        grads_sib.append(difference(sib, jnp.where(to_home_first, second, first)))
        grads_home.append(difference(home, jnp.where(to_home_first, first, second)))
        grads_far.append(swap(grads_sib[m], "rep", 2))
        nears.append(swap(grads_home[m], "rep", 1))
        farthers.append(swap(grads_far[m], "rep", 1))

    state_blocks = [[None] * 4 for _ in range(micro_count)]

    def back(gradient):
        partial = jnp.einsum(
            "rv,wv->rw", gradient, head_weight, preferred_element_type=jnp.float32
        )
        return partial, swap(partial.astype(jnp.bfloat16), "voc", 1)

    held = []
    for part in range(2):
        for m in range(micro_count):
            here, there = ((grads_home, nears), (grads_far, farthers))[part]
            gradient = jnp.concatenate([here[m], there[m]], axis=0)
            partial, sent = back(gradient)
            held.append((m, part, gradient, partial, sent))
    state_parts = []
    for m in range(micro_count):
        summed = [None, None]
        for at, part, gradient, partial, sent in held:
            if at == m:
                summed[part] = (partial + sent.astype(jnp.float32)).astype(jnp.bfloat16)
        canon = [summed[0][:quarter], summed[1][:quarter], summed[0][quarter:], summed[1][quarter:]]
        state_parts.append(
            jnp.einsum(
                "ei,ew->iw",
                onehot[m],
                jnp.concatenate(canon, axis=0),
                preferred_element_type=jnp.float32,
            )
        )
    state_grad = jnp.stack(state_parts).astype(jnp.bfloat16)
    rows, gradients = [], []
    for m, part, gradient, _, _ in held:
        rows += [ordered[m][(2 * b + part) * quarter : (2 * b + part + 1) * quarter] for b in range(2)]
        gradients.append(gradient)
    head_grad = jnp.einsum(
        "rw,rv->wv",
        jnp.concatenate(rows, axis=0),
        jnp.concatenate(gradients, axis=0),
        preferred_element_type=jnp.float32,
    )
    return state_grad, head_grad.astype(jnp.bfloat16)


def spread_body(states, head_weight, pair_order, row_example):
    micro_count, row_count, half_width = states.shape
    devices = lax.axis_size("rep")
    place = lax.axis_index("rep")
    replica, side = place // 2, place % 2
    half = row_count // 2
    local = jnp.arange(row_count, dtype=jnp.int32)
    example_of = (side ^ (local // half)) * half + local % half
    examples = lax.dynamic_index_in_dim(row_example, replica, 1, keepdims=False)
    onehot = (examples[:, None, :] == example_of[None, :, None]).astype(jnp.bfloat16)
    ordered = jnp.einsum("mei,miw->mew", onehot, states, preferred_element_type=jnp.float32)
    ordered = ordered.astype(jnp.bfloat16)
    partner = partner_table(pair_order)
    sources = jnp.arange(devices, dtype=jnp.int32)
    partner_dev = 2 * jnp.repeat(partner, 2, axis=1) + sources % 2
    state_parts, gradients = [], []
    for m in range(micro_count):
        partial = jnp.dot(ordered[m], head_weight, preferred_element_type=jnp.float32)
        logits = (partial[:half] + swap(partial[half:], "rep", 1)).astype(jnp.bfloat16)
        tiles = logits.reshape(devices, half // devices, -1)
        tiles = lax.all_to_all(tiles, "rep", split_axis=0, concat_axis=0, tiled=True)
        mates = (partner_dev[m][:, None] == sources[None, :]).astype(jnp.bfloat16)
        mate_tiles = jnp.einsum("ds,srv->drv", mates, tiles, preferred_element_type=jnp.float32)
        graded = difference(tiles, mate_tiles)
        graded = lax.all_to_all(graded, "rep", split_axis=0, concat_axis=0, tiled=True)
        graded = graded.reshape(half, -1)
        gradient = jnp.concatenate([graded, swap(graded, "rep", 1)], axis=0)
        gradients.append(gradient)
        back = jnp.einsum("rv,wv->rw", gradient, head_weight, preferred_element_type=jnp.float32)
        state_canon = sum_over(back, "voc").astype(jnp.bfloat16)
        state_parts.append(
            jnp.einsum("ei,ew->iw", onehot[m], state_canon, preferred_element_type=jnp.float32)
        )
    state_grad = jnp.stack(state_parts).astype(jnp.bfloat16)
    head_grad = jnp.einsum(
        "mrw,mrv->wv", ordered, jnp.stack(gradients), preferred_element_type=jnp.float32
    )
    return state_grad, head_grad.astype(jnp.bfloat16)


def solution(mesh):
    replicas = mesh.shape["rep"] // 2
    few = replicas % 2 == 0 and math.factorial(replicas // 2) <= max_branches
    few = few and mesh.shape["voc"] == 2
    return jax.shard_map(
        paired_body if few else spread_body,
        mesh=mesh,
        in_specs=(P(None, None, "rep"), P("rep", "voc"), P(), P()),
        out_specs=(P(None, None, "rep"), P("rep", "voc")),
        check_vma=False,
    )
```

```python
import functools
import itertools
import math

import jax
import jax.numpy as jnp
from jax import lax
from jax.experimental import pallas as pl
from jax.experimental.pallas import tpu as pltpu
from jax.sharding import PartitionSpec as P

distill_weight = 0.0625
max_branches = 24


def partner_table(pair_order):
    slot_count = pair_order.shape[1]
    slot_ids = jnp.arange(slot_count, dtype=jnp.int32)
    matches = pair_order[:, None, :] == slot_ids[None, :, None]
    following = jnp.roll(pair_order, -1, axis=1)
    return jnp.sum(jnp.where(matches, following[:, None, :], 0), axis=2)


def route_kernel(order_ref, code_ref, dest, src, color):
    micro_count, replicas = order_ref.shape
    pairs = replicas // 2
    bits = branch_bits(pairs)
    replica = lax.axis_index("rep") // 2
    for m in range(micro_count):
        for k in range(replicas):
            to, frm = order_ref[m, k], order_ref[m, (k + 1) % replicas]
            dest[frm] = to
            src[to] = frm
            color[k] = -1
        for start in range(0, replicas, 2):
            at = jnp.where(color[start] == 1, start + 1, start)
            for _ in range(pairs):
                color[at] = 0
                color[at ^ 1] = 1
                at = src[dest[at ^ 1] ^ 1]
        code = (1 - color[src[replica]]) * 2 + (1 - color[replica])
        for c in (1, 0):
            sigma = []
            place = jnp.int32(0)
            for z in range(pairs):
                leaves = jnp.where(color[2 * z] == c, 2 * z, 2 * z + 1)
                to = dest[leaves] // 2
                smaller = to
                for earlier in sigma:
                    smaller = smaller - jnp.where(earlier < to, 1, 0)
                place = place * (pairs - z) + smaller
                sigma.append(to)
            code = (code << bits) + place
        code_ref[m] = code


def branch_bits(pairs):
    return (math.factorial(pairs) - 1).bit_length()


def routes(pair_order):
    micro_count, replicas = pair_order.shape
    smem = pl.BlockSpec(memory_space=pltpu.SMEM)
    codes = pl.pallas_call(
        route_kernel,
        out_shape=jax.ShapeDtypeStruct((micro_count,), jnp.int32),
        in_specs=[smem],
        out_specs=smem,
        scratch_shapes=[pltpu.SMEM((replicas,), jnp.int32)] * 3,
    )(pair_order)
    bits = branch_bits(replicas // 2)
    mask = (1 << bits) - 1
    found = []
    for m in range(micro_count):
        code = codes[m]
        flags = code >> (2 * bits)
        found.append((code & mask, (code >> bits) & mask, (flags & 1) == 1, flags >= 2))
    return found


def move_pairs(block, branch, pairs, beside, *given):
    def one(sigma, moved, *rest):
        if any(z != to for z, to in enumerate(sigma)):
            route = [(z * 4 + low, to * 4 + low) for z, to in enumerate(sigma) for low in range(4)]
            moved = lax.ppermute(moved, "rep", route)
        return moved, *beside(*rest)

    every = [functools.partial(one, sigma) for sigma in itertools.permutations(range(pairs))]
    return lax.switch(branch, every, block, *given)


def swap(block, axis, bit):
    count = lax.axis_size(axis)
    return lax.ppermute(block, axis, [(i, i ^ bit) for i in range(count)])


def difference(own, other):
    spread = own.astype(jnp.float32) - other.astype(jnp.float32)
    return (distill_weight * spread).astype(jnp.bfloat16)


def sum_over(block, axis):
    if lax.axis_size(axis) == 2:
        return block + swap(block, axis, 1)
    return lax.psum(block, axis)


def after(block, *others):
    return lax.optimization_barrier((block, *others))[0]


def head_kernel(*refs):
    rows_ref, *blocks, out_ref, whole = refs
    height = blocks[0].shape[0]
    for at, block in enumerate(blocks):
        whole[pl.ds(at * height, height), :] = block[...]
    out_ref[...] = lax.dot_general(
        rows_ref[...], whole[...], (((0,), (0,)), ((), ())), preferred_element_type=jnp.float32
    ).astype(out_ref.dtype)


def head_gradient(rows, blocks):
    count, width = rows.shape
    height, vocab = blocks[0].shape
    step = vocab // 4
    return pl.pallas_call(
        head_kernel,
        grid=(vocab // step,),
        out_shape=jax.ShapeDtypeStruct((width, vocab), jnp.bfloat16),
        in_specs=[pl.BlockSpec((count, width), lambda i: (0, 0))]
        + [pl.BlockSpec((height, step), lambda i: (0, i))] * len(blocks),
        out_specs=pl.BlockSpec((width, step), lambda i: (0, i)),
        scratch_shapes=[pltpu.VMEM((count, step), jnp.bfloat16)],
        compiler_params=pltpu.CompilerParams(vmem_limit_bytes=16 << 20),
        cost_estimate=pl.CostEstimate(
            flops=2 * count * width * vocab,
            bytes_accessed=2 * (count * width + count * vocab + width * vocab),
            transcendentals=0,
        ),
    )(rows, *blocks)


def paired_body(states, head_weight, pair_order, row_example):
    micro_count, row_count, half_width = states.shape
    place = lax.axis_index("rep")
    replica, side = place // 2, place % 2
    parity = replica % 2
    pairs = pair_order.shape[1] // 2
    quarter = row_count // 4
    local = jnp.arange(row_count, dtype=jnp.int32)
    block = local // quarter
    by_core = (block >> 1, block & 1)
    by_chip = (block & 1, block >> 1)
    examples = lax.dynamic_index_in_dim(row_example, replica, 1, keepdims=False)

    def onehots(order):
        other_core, other_chip = order
        example_of = (
            (side ^ other_core) * (2 * quarter) + (parity ^ other_chip) * quarter + local % quarter
        )
        return (examples[:, None, :] == example_of[None, :, None]).astype(jnp.bfloat16)

    onehot_core, onehot_chip = onehots(by_core), onehots(by_chip)

    logits = []
    for m in range(micro_count):
        rows = jnp.dot(onehot_core[m], states[m], preferred_element_type=jnp.float32)
        rows = rows.astype(jnp.bfloat16)
        theirs = jnp.dot(rows[2 * quarter :], head_weight, preferred_element_type=jnp.float32)
        arrived = swap(theirs, "rep", 1)
        own = jnp.dot(rows[: 2 * quarter], head_weight, preferred_element_type=jnp.float32)
        far = (own[quarter:] + arrived[quarter:]).astype(jnp.bfloat16)
        home = (own[:quarter] + arrived[:quarter]).astype(jnp.bfloat16)
        logits.append((home, far))
    sib = swap(logits[0][1], "rep", 2)
    codes = routes(after(pair_order, *logits[-1]))
    chip_rows = jnp.einsum(
        "mei,miw->mew", onehot_chip, after(states, *logits[-1]), preferred_element_type=jnp.float32
    )
    chip_rows = chip_rows.astype(jnp.bfloat16)

    def settle(home, sib, first, second, to_home_first):
        grad_home = difference(home, jnp.where(to_home_first, first, second))
        grad_sib = difference(sib, jnp.where(to_home_first, second, first))
        return grad_home, grad_sib

    grads = []
    waiting = None
    for m in range(micro_count):
        home = logits[m][0]
        branch_first, branch_second, home_first, to_home_first = codes[m]
        sent_first = jnp.where(home_first, home, sib)
        sent_second = jnp.where(home_first, sib, home)
        nexts = [logits[m + 1][1]] if m + 1 < micro_count else []

        def beside_first(nexts, waiting):
            arriving = [swap(far, "rep", 2) for far in nexts]
            settled = []
            if waiting is not None:
                settled = settle(*waiting)
                settled = [*settled, swap(settled[0], "rep", 1)]
            return arriving, settled

        def beside_second(back):
            return [swap(grad, "rep", 2) for grad in back]

        first, arriving, settled = move_pairs(
            sent_first, branch_first, pairs, beside_first, nexts, waiting
        )
        back = [settled[1]] if settled else []
        second, *returned = move_pairs(
            after(sent_second, first), branch_second, pairs, beside_second, back
        )
        if settled:
            grads.append([settled[0], settled[2], returned[0]])
        waiting = (home, sib, first, second, to_home_first)
        sib = arriving[0] if arriving else None
    grad_home, grad_sib = settle(*waiting)
    grads.append([grad_home, swap(grad_home, "rep", 1), swap(grad_sib, "rep", 2)])
    for group in grads:
        group.append(swap(group[2], "rep", 1))

    def back(first, second):
        gradient = jnp.concatenate([first, second], axis=0)
        partial = jnp.einsum(
            "rv,wv->rw", gradient, head_weight, preferred_element_type=jnp.float32
        )
        return partial + swap(partial.astype(jnp.bfloat16), "voc", 1).astype(jnp.float32)

    state_parts = []
    for m in range(micro_count):
        near, far = back(*grads[m][:2]), back(*grads[m][2:])
        state_parts.append(
            jnp.einsum(
                "ei,ew->iw",
                onehot_chip[m],
                jnp.concatenate([near, far], axis=0).astype(jnp.bfloat16),
                preferred_element_type=jnp.float32,
            )
        )
    state_grad = jnp.stack(state_parts).astype(jnp.bfloat16)
    head_grad = head_gradient(
        chip_rows.reshape(micro_count * row_count, half_width), sum(grads, [])
    )
    return state_grad, head_grad


def spread_body(states, head_weight, pair_order, row_example):
    micro_count, row_count, half_width = states.shape
    devices = lax.axis_size("rep")
    place = lax.axis_index("rep")
    replica, side = place // 2, place % 2
    half = row_count // 2
    local = jnp.arange(row_count, dtype=jnp.int32)
    example_of = (side ^ (local // half)) * half + local % half
    examples = lax.dynamic_index_in_dim(row_example, replica, 1, keepdims=False)
    onehot = (examples[:, None, :] == example_of[None, :, None]).astype(jnp.bfloat16)
    ordered = jnp.einsum("mei,miw->mew", onehot, states, preferred_element_type=jnp.float32)
    ordered = ordered.astype(jnp.bfloat16)
    partner = partner_table(pair_order)
    sources = jnp.arange(devices, dtype=jnp.int32)
    partner_dev = 2 * jnp.repeat(partner, 2, axis=1) + sources % 2
    state_parts, gradients = [], []
    for m in range(micro_count):
        partial = jnp.dot(ordered[m], head_weight, preferred_element_type=jnp.float32)
        logits = (partial[:half] + swap(partial[half:], "rep", 1)).astype(jnp.bfloat16)
        tiles = logits.reshape(devices, half // devices, -1)
        tiles = lax.all_to_all(tiles, "rep", split_axis=0, concat_axis=0, tiled=True)
        mates = (partner_dev[m][:, None] == sources[None, :]).astype(jnp.bfloat16)
        mate_tiles = jnp.einsum("ds,srv->drv", mates, tiles, preferred_element_type=jnp.float32)
        graded = difference(tiles, mate_tiles)
        graded = lax.all_to_all(graded, "rep", split_axis=0, concat_axis=0, tiled=True)
        graded = graded.reshape(half, -1)
        gradient = jnp.concatenate([graded, swap(graded, "rep", 1)], axis=0)
        gradients.append(gradient)
        back = jnp.einsum("rv,wv->rw", gradient, head_weight, preferred_element_type=jnp.float32)
        state_canon = sum_over(back, "voc").astype(jnp.bfloat16)
        state_parts.append(
            jnp.einsum("ei,ew->iw", onehot[m], state_canon, preferred_element_type=jnp.float32)
        )
    state_grad = jnp.stack(state_parts).astype(jnp.bfloat16)
    head_grad = jnp.einsum(
        "mrw,mrv->wv", ordered, jnp.stack(gradients), preferred_element_type=jnp.float32
    )
    return state_grad, head_grad.astype(jnp.bfloat16)


def solution(mesh):
    replicas = mesh.shape["rep"] // 2
    few = replicas % 2 == 0 and math.factorial(replicas // 2) <= max_branches
    few = few and mesh.shape["voc"] == 2
    return jax.shard_map(
        paired_body if few else spread_body,
        mesh=mesh,
        in_specs=(P(None, None, "rep"), P("rep", "voc"), P(), P()),
        out_specs=(P(None, None, "rep"), P("rep", "voc")),
        check_vma=False,
    )
```

```python
import functools
import itertools
import math

import jax
import jax.numpy as jnp
from jax import lax
from jax.experimental import pallas as pl
from jax.experimental.pallas import tpu as pltpu
from jax.sharding import PartitionSpec as P

distill_weight = 0.0625
max_permutations = 24


def partner_table(pair_order):
    slot_count = pair_order.shape[1]
    slot_ids = jnp.arange(slot_count, dtype=jnp.int32)
    matches = pair_order[:, None, :] == slot_ids[None, :, None]
    following = jnp.roll(pair_order, -1, axis=1)
    return jnp.sum(jnp.where(matches, following[:, None, :], 0), axis=2)


def route_kernel(order_ref, *refs):
    *branch_refs, flags_ref, dest, src, color = refs
    micro_count, replicas = order_ref.shape
    pairs = replicas // 2
    replica = lax.axis_index("rep") // 2
    for m in range(micro_count):
        for k in range(replicas):
            to, frm = order_ref[m, k], order_ref[m, (k + 1) % replicas]
            dest[frm] = to
            src[to] = frm
            color[k] = -1
        for start in range(0, replicas, 2):
            at = jnp.where(color[start] == 1, start + 1, start)
            for _ in range(pairs):
                color[at] = 0
                color[at ^ 1] = 1
                at = src[dest[at ^ 1] ^ 1]
        for c in range(2):
            sigma = []
            place = jnp.int32(0)
            for z in range(pairs):
                leaves = jnp.where(color[2 * z] == c, 2 * z, 2 * z + 1)
                to = dest[leaves] // 2
                smaller = to
                for earlier in sigma:
                    smaller = smaller - jnp.where(earlier < to, 1, 0)
                place = place * (pairs - z) + smaller
                sigma.append(to)
            branch_refs[2 * m + c][0] = place
        for row, moved in enumerate((replica, src[replica])):
            at = 2 * m + row
            flags_ref[at : at + 1, :] = jnp.full((1, flags_ref.shape[1]), color[moved], jnp.int32)


def routes(pair_order):
    micro_count, replicas = pair_order.shape
    smem = pl.BlockSpec(memory_space=pltpu.SMEM)
    *branches, flags = pl.pallas_call(
        route_kernel,
        out_shape=[jax.ShapeDtypeStruct((1,), jnp.int32)] * (2 * micro_count)
        + [jax.ShapeDtypeStruct((2 * micro_count, 128), jnp.int32)],
        in_specs=[smem],
        out_specs=[smem] * (2 * micro_count) + [pl.BlockSpec(memory_space=pltpu.VMEM)],
        scratch_shapes=[pltpu.SMEM((replicas,), jnp.int32)] * 3,
        compiler_params=pltpu.CompilerParams(vmem_limit_bytes=1 << 20),
    )(pair_order)
    branch = [number.reshape(()) for number in branches]
    flag = [flags[at : at + 1, :1] == 0 for at in range(2 * micro_count)]
    return [(branch[2 * m : 2 * m + 2], flag[2 * m : 2 * m + 2]) for m in range(micro_count)]


def move_pairs(block, branch, pairs, beside, *given):
    def one(sigma, moved, *rest):
        if any(z != to for z, to in enumerate(sigma)):
            route = [(z * 4 + low, to * 4 + low) for z, to in enumerate(sigma) for low in range(4)]
            moved = lax.ppermute(moved, "rep", route)
        return moved, beside(*rest)

    every = [functools.partial(one, sigma) for sigma in itertools.permutations(range(pairs))]
    return lax.switch(branch, every, block, *given)


def swap(block, axis, bit):
    count = lax.axis_size(axis)
    return lax.ppermute(block, axis, [(i, i ^ bit) for i in range(count)])


def difference(own, other):
    spread = own.astype(jnp.float32) - other.astype(jnp.float32)
    return (distill_weight * spread).astype(jnp.bfloat16)


def sum_over(block, axis):
    if lax.axis_size(axis) == 2:
        return block + swap(block, axis, 1)
    return lax.psum(block, axis)


def after(block, *others):
    return lax.optimization_barrier((block, *others))[0]


def head_kernel(*refs):
    rows_ref, *blocks, out_ref, whole = refs
    height = blocks[0].shape[0]
    for at, block in enumerate(blocks):
        whole[pl.ds(at * height, height), :] = block[...]
    out_ref[...] = lax.dot_general(
        rows_ref[...], whole[...], (((0,), (0,)), ((), ())), preferred_element_type=jnp.float32
    ).astype(out_ref.dtype)


def head_gradient(rows, blocks):
    count, width = rows.shape
    height, vocab = blocks[0].shape
    step = vocab // 4
    return pl.pallas_call(
        head_kernel,
        grid=(vocab // step,),
        out_shape=jax.ShapeDtypeStruct((width, vocab), jnp.bfloat16),
        in_specs=[pl.BlockSpec((count, width), lambda i: (0, 0))]
        + [pl.BlockSpec((height, step), lambda i: (0, i))] * len(blocks),
        out_specs=pl.BlockSpec((width, step), lambda i: (0, i)),
        scratch_shapes=[pltpu.VMEM((count, step), jnp.bfloat16)],
        compiler_params=pltpu.CompilerParams(vmem_limit_bytes=16 << 20),
        cost_estimate=pl.CostEstimate(
            flops=2 * count * width * vocab,
            bytes_accessed=2 * (count * width + count * vocab + width * vocab),
            transcendentals=0,
        ),
    )(rows, *blocks)


def paired_body(states, head_weight, pair_order, row_example):
    micro_count, row_count, half_width = states.shape
    place = lax.axis_index("rep")
    replica, side = place // 2, place % 2
    parity = replica % 2
    pairs = pair_order.shape[1] // 2
    quarter = row_count // 4
    local = jnp.arange(row_count, dtype=jnp.int32)
    block = local // quarter
    by_core = (block >> 1, block & 1)
    by_chip = (block & 1, block >> 1)
    examples = lax.dynamic_index_in_dim(row_example, replica, 1, keepdims=False)

    def onehots(order):
        other_core, other_chip = order
        example_of = (
            (side ^ other_core) * (2 * quarter) + (parity ^ other_chip) * quarter + local % quarter
        )
        return (examples[:, None, :] == example_of[None, :, None]).astype(jnp.bfloat16)

    onehot_core, onehot_chip = onehots(by_core), onehots(by_chip)

    logits = []
    for m in range(micro_count):
        rows = jnp.dot(onehot_core[m], states[m], preferred_element_type=jnp.float32)
        rows = rows.astype(jnp.bfloat16)
        theirs = jnp.dot(rows[2 * quarter :], head_weight, preferred_element_type=jnp.float32)
        arrived = swap(theirs, "rep", 1)
        own = jnp.dot(rows[: 2 * quarter], head_weight, preferred_element_type=jnp.float32)
        far = (own[quarter:] + arrived[quarter:]).astype(jnp.bfloat16)
        home = (own[:quarter] + arrived[:quarter]).astype(jnp.bfloat16)
        logits.append((home, far))
    sib = swap(logits[0][1], "rep", 2)
    codes = routes(after(pair_order, *logits[-1]))
    chip_rows = jnp.einsum(
        "mei,miw->mew", onehot_chip, after(states, *logits[-1]), preferred_element_type=jnp.float32
    )
    chip_rows = chip_rows.astype(jnp.bfloat16)

    def settle(home, sib, first, second, to_home_first):
        grad_home = difference(home, jnp.where(to_home_first, first, second))
        grad_sib = difference(sib, jnp.where(to_home_first, second, first))
        return grad_home, grad_sib

    def leaving(home, sib, home_first):
        return jnp.where(home_first, home, sib), jnp.where(home_first, sib, home)

    def first_beside(far, waiting):
        return [swap(block, "rep", 2) for block in far], [settle(*group) for group in waiting]

    def second_beside(coming, settled):
        sent = [leaving(*group) for group in coming]
        returned = []
        for grad_home, grad_sib in settled:
            grad_far = swap(grad_sib, "rep", 2)
            near = swap(grad_home, "rep", 1)
            returned.append([grad_home, near, grad_far, swap(grad_far, "rep", 1)])
        return sent, returned

    grads, waiting = [], []
    (branches, (home_first, to_home_first)) = codes[0]
    home = logits[0][0]
    sent = leaving(home, sib, home_first)
    for m in range(micro_count):
        last = m + 1 == micro_count
        first, (arrived, settled) = move_pairs(
            sent[0], branches[0], pairs, first_beside, [] if last else [logits[m + 1][1]], waiting
        )
        coming = [] if last else [(logits[m + 1][0], arrived[0], codes[m + 1][1][0])]
        second, (sents, returned) = move_pairs(
            after(sent[1], first), branches[1], pairs, second_beside, coming, settled
        )
        grads += returned
        waiting = [(home, sib, first, second, to_home_first)]
        if not last:
            (branches, (home_first, to_home_first)) = codes[m + 1]
            home, sib, sent = logits[m + 1][0], arrived[0], sents[0]
    [(grad_home, grad_sib)] = [settle(*group) for group in waiting]
    grad_far = swap(grad_sib, "rep", 2)
    near = swap(grad_home, "rep", 1)
    grads = [[after(block, near) for block in group] for group in grads]
    grads.append([grad_home, near, grad_far, swap(grad_far, "rep", 1)])

    def back(first, second):
        gradient = jnp.concatenate([first, second], axis=0)
        partial = jnp.einsum(
            "rv,wv->rw", gradient, head_weight, preferred_element_type=jnp.float32
        )
        return partial + swap(partial.astype(jnp.bfloat16), "voc", 1).astype(jnp.float32)

    canon = []
    for group in grads:
        near, far = back(*group[:2]), back(*group[2:])
        canon.append(jnp.concatenate([near, far], axis=0).astype(jnp.bfloat16))
    state_grad = jnp.einsum(
        "mei,mew->miw", onehot_chip, jnp.stack(canon), preferred_element_type=jnp.float32
    ).astype(jnp.bfloat16)
    head_grad = head_gradient(
        chip_rows.reshape(micro_count * row_count, half_width), sum(grads, [])
    )
    return state_grad, head_grad


def spread_body(states, head_weight, pair_order, row_example):
    micro_count, row_count, half_width = states.shape
    devices = lax.axis_size("rep")
    place = lax.axis_index("rep")
    replica, side = place // 2, place % 2
    half = row_count // 2
    local = jnp.arange(row_count, dtype=jnp.int32)
    example_of = (side ^ (local // half)) * half + local % half
    examples = lax.dynamic_index_in_dim(row_example, replica, 1, keepdims=False)
    onehot = (examples[:, None, :] == example_of[None, :, None]).astype(jnp.bfloat16)
    ordered = jnp.einsum("mei,miw->mew", onehot, states, preferred_element_type=jnp.float32)
    ordered = ordered.astype(jnp.bfloat16)
    partner = partner_table(pair_order)
    sources = jnp.arange(devices, dtype=jnp.int32)
    partner_dev = 2 * jnp.repeat(partner, 2, axis=1) + sources % 2
    state_parts, gradients = [], []
    for m in range(micro_count):
        partial = jnp.dot(ordered[m], head_weight, preferred_element_type=jnp.float32)
        logits = (partial[:half] + swap(partial[half:], "rep", 1)).astype(jnp.bfloat16)
        tiles = logits.reshape(devices, half // devices, -1)
        tiles = lax.all_to_all(tiles, "rep", split_axis=0, concat_axis=0, tiled=True)
        mates = (partner_dev[m][:, None] == sources[None, :]).astype(jnp.bfloat16)
        mate_tiles = jnp.einsum("ds,srv->drv", mates, tiles, preferred_element_type=jnp.float32)
        graded = difference(tiles, mate_tiles)
        graded = lax.all_to_all(graded, "rep", split_axis=0, concat_axis=0, tiled=True)
        graded = graded.reshape(half, -1)
        gradient = jnp.concatenate([graded, swap(graded, "rep", 1)], axis=0)
        gradients.append(gradient)
        back = jnp.einsum("rv,wv->rw", gradient, head_weight, preferred_element_type=jnp.float32)
        state_canon = sum_over(back, "voc").astype(jnp.bfloat16)
        state_parts.append(
            jnp.einsum("ei,ew->iw", onehot[m], state_canon, preferred_element_type=jnp.float32)
        )
    state_grad = jnp.stack(state_parts).astype(jnp.bfloat16)
    head_grad = jnp.einsum(
        "mrw,mrv->wv", ordered, jnp.stack(gradients), preferred_element_type=jnp.float32
    )
    return state_grad, head_grad.astype(jnp.bfloat16)


def solution(mesh):
    replicas = mesh.shape["rep"] // 2
    few = replicas % 2 == 0 and math.factorial(replicas // 2) <= max_permutations
    few = few and mesh.shape["voc"] == 2
    return jax.shard_map(
        paired_body if few else spread_body,
        mesh=mesh,
        in_specs=(P(None, None, "rep"), P("rep", "voc"), P(), P()),
        out_specs=(P(None, None, "rep"), P("rep", "voc")),
        check_vma=False,
    )
```

```python
import functools
import itertools
import math

import jax
import jax.numpy as jnp
import numpy as np
from jax import lax
from jax.experimental import pallas as pl
from jax.experimental.pallas import tpu as pltpu
from jax.sharding import PartitionSpec as P

distill_weight = 0.0625
max_permutations = 24


def partner_table(pair_order):
    slot_count = pair_order.shape[1]
    slot_ids = jnp.arange(slot_count, dtype=jnp.int32)
    matches = pair_order[:, None, :] == slot_ids[None, :, None]
    following = jnp.roll(pair_order, -1, axis=1)
    return jnp.sum(jnp.where(matches, following[:, None, :], 0), axis=2)


@functools.cache
def permutation_pairs(pairs):
    every = list(itertools.permutations(range(pairs)))
    found = []
    for at, first in enumerate(every):
        partners = []
        for later in range(at, len(every)):
            group = list(range(pairs))
            for sigma in (first, every[later]):
                for z, to in enumerate(sigma):
                    group = [group[z] if g == group[to] else g for g in group]
            if len(set(group)) == 1:
                partners.append(later)
        found.append(partners)
    return every, found


def pair_codes(pairs):
    every, found = permutation_pairs(pairs)
    codes = np.zeros((len(every), len(every)), np.int32)
    for at, partners in enumerate(found):
        for rank, later in enumerate(partners):
            codes[at, later] = codes[later, at] = rank
    return codes.reshape(-1)


def route_kernel(order_ref, codes_ref, *refs):
    *branch_refs, flags_ref, dest, src, color = refs
    micro_count, replicas = order_ref.shape
    pairs = replicas // 2
    replica = lax.axis_index("rep") // 2
    for m in range(micro_count):
        for k in range(replicas):
            to, frm = order_ref[m, k], order_ref[m, (k + 1) % replicas]
            dest[frm] = to
            src[to] = frm
            color[k] = -1
        for start in range(0, replicas, 2):
            at = jnp.where(color[start] == 1, start + 1, start)
            for _ in range(pairs):
                color[at] = 0
                color[at ^ 1] = 1
                at = src[dest[at ^ 1] ^ 1]
        places = []
        for c in range(2):
            sigma = []
            place = jnp.int32(0)
            for z in range(pairs):
                leaves = jnp.where(color[2 * z] == c, 2 * z, 2 * z + 1)
                to = dest[leaves] // 2
                smaller = to
                for earlier in sigma:
                    smaller = smaller - jnp.where(earlier < to, 1, 0)
                place = place * (pairs - z) + smaller
                sigma.append(to)
            places.append(place)
        branch_refs[2 * m][0] = jnp.minimum(*places)
        branch_refs[2 * m + 1][0] = codes_ref[places[0] * math.factorial(pairs) + places[1]]
        first_color = jnp.where(places[0] <= places[1], 0, 1)
        for row, moved in enumerate((replica, src[replica])):
            at = 2 * m + row
            flag = jnp.where(color[moved] == first_color, 0, 1)
            flags_ref[at : at + 1, :] = jnp.full((1, flags_ref.shape[1]), flag, jnp.int32)


def routes(pair_order, width):
    micro_count, replicas = pair_order.shape
    smem = pl.BlockSpec(memory_space=pltpu.SMEM)
    *branches, flags = pl.pallas_call(
        route_kernel,
        out_shape=[jax.ShapeDtypeStruct((1,), jnp.int32)] * (2 * micro_count)
        + [jax.ShapeDtypeStruct((2 * micro_count, width), jnp.int32)],
        in_specs=[smem, smem],
        out_specs=[smem] * (2 * micro_count) + [pl.BlockSpec(memory_space=pltpu.VMEM)],
        scratch_shapes=[pltpu.SMEM((replicas,), jnp.int32)] * 3,
        compiler_params=pltpu.CompilerParams(vmem_limit_bytes=1 << 20),
    )(pair_order, jnp.asarray(pair_codes(replicas // 2)))
    branch = [number.reshape(()) for number in branches]
    flag = [flags[at : at + 1] == 0 for at in range(2 * micro_count)]
    return [(branch[2 * m : 2 * m + 2], flag[2 * m : 2 * m + 2]) for m in range(micro_count)]


def move_pairs(first, second, branch, pairs, beside, *given):
    every, partners = permutation_pairs(pairs)

    def by(sigma, block):
        if all(z == to for z, to in enumerate(sigma)):
            return block
        route = [(z * 4 + low, to * 4 + low) for z, to in enumerate(sigma) for low in range(4)]
        return lax.ppermute(block, "rep", route)

    def outer(at, first, second, later, *rest):
        moved = by(every[at], first)
        early, late = beside(*rest)
        inner = [functools.partial(by, every[partner]) for partner in partners[at]]
        return moved, lax.switch(later, inner, after(second, *early)), late

    places = range(len(every) - [bool(p) for p in partners][::-1].index(True))
    branches = [functools.partial(outer, at) if partners[at] else None for at in places]
    some = next(b for b in branches if b)
    return lax.switch(branch[0], [b or some for b in branches], first, second, branch[1], *given)


def swap(block, axis, bit):
    count = lax.axis_size(axis)
    return lax.ppermute(block, axis, [(i, i ^ bit) for i in range(count)])


def difference(own, other):
    spread = own.astype(jnp.float32) - other.astype(jnp.float32)
    return (distill_weight * spread).astype(jnp.bfloat16)


def sum_over(block, axis):
    if lax.axis_size(axis) == 2:
        return block + swap(block, axis, 1)
    return lax.psum(block, axis)


def after(block, *others):
    return lax.optimization_barrier((block, *others))[0]


def head_kernel(*refs):
    rows_ref, *blocks, out_ref, whole = refs
    height = blocks[0].shape[0]
    for at, block in enumerate(blocks):
        whole[pl.ds(at * height, height), :] = block[...]
    out_ref[...] = lax.dot_general(
        rows_ref[...], whole[...], (((0,), (0,)), ((), ())), preferred_element_type=jnp.float32
    ).astype(out_ref.dtype)


def head_gradient(rows, blocks):
    count, width = rows.shape
    height, vocab = blocks[0].shape
    step = vocab // 4
    return pl.pallas_call(
        head_kernel,
        grid=(vocab // step,),
        out_shape=jax.ShapeDtypeStruct((width, vocab), jnp.bfloat16),
        in_specs=[pl.BlockSpec((count, width), lambda i: (0, 0))]
        + [pl.BlockSpec((height, step), lambda i: (0, i))] * len(blocks),
        out_specs=pl.BlockSpec((width, step), lambda i: (0, i)),
        scratch_shapes=[pltpu.VMEM((count, step), jnp.bfloat16)],
        compiler_params=pltpu.CompilerParams(vmem_limit_bytes=16 << 20),
        cost_estimate=pl.CostEstimate(
            flops=2 * count * width * vocab,
            bytes_accessed=2 * (count * width + count * vocab + width * vocab),
            transcendentals=0,
        ),
    )(rows, *blocks)


def paired_body(states, head_weight, pair_order, row_example):
    micro_count, row_count, half_width = states.shape
    place = lax.axis_index("rep")
    replica, side = place // 2, place % 2
    parity = replica % 2
    pairs = pair_order.shape[1] // 2
    quarter = row_count // 4
    local = jnp.arange(row_count, dtype=jnp.int32)
    block = local // quarter
    by_core = (block >> 1, block & 1)
    by_chip = (block & 1, block >> 1)
    examples = lax.dynamic_index_in_dim(row_example, replica, 1, keepdims=False)

    def onehots(order):
        other_core, other_chip = order
        example_of = (
            (side ^ other_core) * (2 * quarter) + (parity ^ other_chip) * quarter + local % quarter
        )
        return (examples[:, None, :] == example_of[None, :, None]).astype(jnp.bfloat16)

    onehot_core, onehot_chip = onehots(by_core), onehots(by_chip)

    logits = []
    for m in range(micro_count):
        rows = jnp.dot(onehot_core[m], states[m], preferred_element_type=jnp.float32)
        rows = rows.astype(jnp.bfloat16)
        theirs = jnp.dot(rows[2 * quarter :], head_weight, preferred_element_type=jnp.float32)
        arrived = swap(theirs, "rep", 1)
        own = jnp.dot(rows[: 2 * quarter], head_weight, preferred_element_type=jnp.float32)
        far = (own[quarter:] + arrived[quarter:]).astype(jnp.bfloat16)
        home = (own[:quarter] + arrived[:quarter]).astype(jnp.bfloat16)
        logits.append((home, far))
    sib = swap(logits[0][1], "rep", 2)
    codes = routes(after(pair_order, *logits[-1]), head_weight.shape[1])
    chip_rows = jnp.einsum(
        "mei,miw->mew", onehot_chip, after(states, *logits[-1]), preferred_element_type=jnp.float32
    )
    chip_rows = chip_rows.astype(jnp.bfloat16)

    def settle(home, sib, first, second, to_home_first):
        grad_home = difference(home, jnp.where(to_home_first, first, second))
        grad_sib = difference(sib, jnp.where(to_home_first, second, first))
        return grad_home, grad_sib

    def leaving(home, sib, home_first):
        return jnp.where(home_first, home, sib), jnp.where(home_first, sib, home)

    def beside(nexts, waiting):
        arriving = [swap(far, "rep", 2) for far in nexts]
        returned, early = [], []
        for group in waiting:
            grad_home, grad_sib = settle(*group)
            returned.append([grad_home, swap(grad_home, "rep", 1), swap(grad_sib, "rep", 2)])
            early += [grad_home, grad_sib]
        return early, (arriving, returned)

    grads, waiting = [], []
    for m in range(micro_count):
        home = logits[m][0]
        branch, (home_first, to_home_first) = codes[m]
        nexts = [] if m + 1 == micro_count else [logits[m + 1][1]]
        first, second, (arriving, returned) = move_pairs(
            *leaving(home, sib, home_first), branch, pairs, beside, nexts, waiting
        )
        grads += returned
        waiting = [(home, sib, first, second, to_home_first)]
        sib = arriving[0] if arriving else None
    [(grad_home, grad_sib)] = [settle(*group) for group in waiting]
    grad_far = swap(grad_sib, "rep", 2)
    near = swap(grad_home, "rep", 1)
    grads = [[after(block, near) for block in group] for group in grads]
    grads.append([grad_home, near, grad_far])
    for group in grads:
        group.append(swap(group[2], "rep", 1))

    def back(first, second):
        gradient = jnp.concatenate([first, second], axis=0)
        partial = jnp.einsum(
            "rv,wv->rw", gradient, head_weight, preferred_element_type=jnp.float32
        )
        return partial + swap(partial.astype(jnp.bfloat16), "voc", 1).astype(jnp.float32)

    canon = []
    for group in grads:
        near, far = back(*group[:2]), back(*group[2:])
        canon.append(jnp.concatenate([near, far], axis=0).astype(jnp.bfloat16))
    state_grad = jnp.einsum(
        "mei,mew->miw", onehot_chip, jnp.stack(canon), preferred_element_type=jnp.float32
    ).astype(jnp.bfloat16)
    head_grad = head_gradient(
        chip_rows.reshape(micro_count * row_count, half_width), sum(grads, [])
    )
    return state_grad, head_grad


def spread_body(states, head_weight, pair_order, row_example):
    micro_count, row_count, half_width = states.shape
    devices = lax.axis_size("rep")
    place = lax.axis_index("rep")
    replica, side = place // 2, place % 2
    half = row_count // 2
    local = jnp.arange(row_count, dtype=jnp.int32)
    example_of = (side ^ (local // half)) * half + local % half
    examples = lax.dynamic_index_in_dim(row_example, replica, 1, keepdims=False)
    onehot = (examples[:, None, :] == example_of[None, :, None]).astype(jnp.bfloat16)
    ordered = jnp.einsum("mei,miw->mew", onehot, states, preferred_element_type=jnp.float32)
    ordered = ordered.astype(jnp.bfloat16)
    partner = partner_table(pair_order)
    sources = jnp.arange(devices, dtype=jnp.int32)
    partner_dev = 2 * jnp.repeat(partner, 2, axis=1) + sources % 2
    state_parts, gradients = [], []
    for m in range(micro_count):
        partial = jnp.dot(ordered[m], head_weight, preferred_element_type=jnp.float32)
        logits = (partial[:half] + swap(partial[half:], "rep", 1)).astype(jnp.bfloat16)
        tiles = logits.reshape(devices, half // devices, -1)
        tiles = lax.all_to_all(tiles, "rep", split_axis=0, concat_axis=0, tiled=True)
        mates = (partner_dev[m][:, None] == sources[None, :]).astype(jnp.bfloat16)
        mate_tiles = jnp.einsum("ds,srv->drv", mates, tiles, preferred_element_type=jnp.float32)
        graded = difference(tiles, mate_tiles)
        graded = lax.all_to_all(graded, "rep", split_axis=0, concat_axis=0, tiled=True)
        graded = graded.reshape(half, -1)
        gradient = jnp.concatenate([graded, swap(graded, "rep", 1)], axis=0)
        gradients.append(gradient)
        back = jnp.einsum("rv,wv->rw", gradient, head_weight, preferred_element_type=jnp.float32)
        state_canon = sum_over(back, "voc").astype(jnp.bfloat16)
        state_parts.append(
            jnp.einsum("ei,ew->iw", onehot[m], state_canon, preferred_element_type=jnp.float32)
        )
    state_grad = jnp.stack(state_parts).astype(jnp.bfloat16)
    head_grad = jnp.einsum(
        "mrw,mrv->wv", ordered, jnp.stack(gradients), preferred_element_type=jnp.float32
    )
    return state_grad, head_grad.astype(jnp.bfloat16)


def solution(mesh):
    replicas = mesh.shape["rep"] // 2
    few = replicas % 2 == 0 and math.factorial(replicas // 2) <= max_permutations
    few = few and mesh.shape["voc"] == 2
    return jax.shard_map(
        paired_body if few else spread_body,
        mesh=mesh,
        in_specs=(P(None, None, "rep"), P("rep", "voc"), P(), P()),
        out_specs=(P(None, None, "rep"), P("rep", "voc")),
        check_vma=False,
    )
```

```python
import functools
import itertools
import math

import jax
import jax.numpy as jnp
from jax import lax
from jax.experimental import pallas as pl
from jax.experimental.pallas import tpu as pltpu
from jax.sharding import PartitionSpec as P

distill_weight = 0.0625
max_permutations = 24


def partner_table(pair_order):
    slot_count = pair_order.shape[1]
    slot_ids = jnp.arange(slot_count, dtype=jnp.int32)
    matches = pair_order[:, None, :] == slot_ids[None, :, None]
    following = jnp.roll(pair_order, -1, axis=1)
    return jnp.sum(jnp.where(matches, following[:, None, :], 0), axis=2)


def route_kernel(order_ref, *refs):
    *branch_refs, flags_ref, dest, src, color = refs
    micro_count, replicas = order_ref.shape
    pairs = replicas // 2
    replica = lax.axis_index("rep") // 2
    for m in range(micro_count):
        for k in range(replicas):
            to, frm = order_ref[m, k], order_ref[m, (k + 1) % replicas]
            dest[frm] = to
            src[to] = frm
            color[k] = -1
        for start in range(0, replicas, 2):
            at = jnp.where(color[start] == 1, start + 1, start)
            for _ in range(pairs):
                color[at] = 0
                color[at ^ 1] = 1
                at = src[dest[at ^ 1] ^ 1]
        for c in range(2):
            sigma = []
            place = jnp.int32(0)
            for z in range(pairs):
                leaves = jnp.where(color[2 * z] == c, 2 * z, 2 * z + 1)
                to = dest[leaves] // 2
                smaller = to
                for earlier in sigma:
                    smaller = smaller - jnp.where(earlier < to, 1, 0)
                place = place * (pairs - z) + smaller
                sigma.append(to)
            branch_refs[2 * m + c][0] = place
        for row, moved in enumerate((replica, src[replica])):
            at = 2 * m + row
            flags_ref[at : at + 1, :] = jnp.full((1, flags_ref.shape[1]), color[moved], jnp.int32)


def routes(pair_order, width):
    micro_count, replicas = pair_order.shape
    smem = pl.BlockSpec(memory_space=pltpu.SMEM)
    *branches, flags = pl.pallas_call(
        route_kernel,
        out_shape=[jax.ShapeDtypeStruct((1,), jnp.int32)] * (2 * micro_count)
        + [jax.ShapeDtypeStruct((2 * micro_count, width), jnp.int32)],
        in_specs=[smem],
        out_specs=[smem] * (2 * micro_count) + [pl.BlockSpec(memory_space=pltpu.VMEM)],
        scratch_shapes=[pltpu.SMEM((replicas,), jnp.int32)] * 3,
        compiler_params=pltpu.CompilerParams(vmem_limit_bytes=1 << 20),
    )(pair_order)
    branch = [number.reshape(()) for number in branches]
    flag = [flags[at : at + 1] == 0 for at in range(2 * micro_count)]
    return [(branch[2 * m : 2 * m + 2], flag[2 * m : 2 * m + 2]) for m in range(micro_count)]


def move_pairs(block, branch, pairs, beside, *given):
    def one(sigma, moved, *rest):
        if any(z != to for z, to in enumerate(sigma)):
            route = [(z * 4 + low, to * 4 + low) for z, to in enumerate(sigma) for low in range(4)]
            moved = lax.ppermute(moved, "rep", route)
        return moved, beside(*rest)

    every = [functools.partial(one, sigma) for sigma in itertools.permutations(range(pairs))]
    return lax.switch(branch, every, block, *given)


def swap(block, axis, bit):
    count = lax.axis_size(axis)
    return lax.ppermute(block, axis, [(i, i ^ bit) for i in range(count)])


def difference(own, other):
    spread = own.astype(jnp.float32) - other.astype(jnp.float32)
    return (distill_weight * spread).astype(jnp.bfloat16)


def sum_over(block, axis):
    if lax.axis_size(axis) == 2:
        return block + swap(block, axis, 1)
    return lax.psum(block, axis)


def after(block, *others):
    return lax.optimization_barrier((block, *others))[0]


def head_kernel(*refs):
    rows_ref, *blocks, out_ref, whole = refs
    height = blocks[0].shape[0]
    for at, block in enumerate(blocks):
        whole[pl.ds(at * height, height), :] = block[...]
    out_ref[...] = lax.dot_general(
        rows_ref[...], whole[...], (((0,), (0,)), ((), ())), preferred_element_type=jnp.float32
    ).astype(out_ref.dtype)


def head_gradient(rows, blocks):
    count, width = rows.shape
    vocab = blocks[0].shape[1]
    return pl.pallas_call(
        head_kernel,
        out_shape=jax.ShapeDtypeStruct((width, vocab), jnp.bfloat16),
        scratch_shapes=[pltpu.VMEM((count, vocab), jnp.bfloat16)],
        compiler_params=pltpu.CompilerParams(vmem_limit_bytes=24 << 20),
        cost_estimate=pl.CostEstimate(
            flops=2 * count * width * vocab,
            bytes_accessed=2 * (count * width + count * vocab + width * vocab),
            transcendentals=0,
        ),
    )(rows, *blocks)


def after(block, *others):
    return lax.optimization_barrier((block, *others))[0]


def head_kernel(*refs):
    rows_ref, *blocks, out_ref, whole = refs
    height = blocks[0].shape[0]
    for at, block in enumerate(blocks):
        whole[pl.ds(at * height, height), :] = block[...]
    out_ref[...] = lax.dot_general(
        rows_ref[...], whole[...], (((0,), (0,)), ((), ())), preferred_element_type=jnp.float32
    ).astype(out_ref.dtype)


def head_gradient(rows, blocks):
    count, width = rows.shape
    height, vocab = blocks[0].shape
    step = vocab // 4
    return pl.pallas_call(
        head_kernel,
        grid=(vocab // step,),
        out_shape=jax.ShapeDtypeStruct((width, vocab), jnp.bfloat16),
        in_specs=[pl.BlockSpec((count, width), lambda i: (0, 0))]
        + [pl.BlockSpec((height, step), lambda i: (0, i))] * len(blocks),
        out_specs=pl.BlockSpec((width, step), lambda i: (0, i)),
        scratch_shapes=[pltpu.VMEM((count, step), jnp.bfloat16)],
        compiler_params=pltpu.CompilerParams(vmem_limit_bytes=16 << 20),
        cost_estimate=pl.CostEstimate(
            flops=2 * count * width * vocab,
            bytes_accessed=2 * (count * width + count * vocab + width * vocab),
            transcendentals=0,
        ),
    )(rows, *blocks)


def paired_body(states, head_weight, pair_order, row_example):
    micro_count, row_count, half_width = states.shape
    place = lax.axis_index("rep")
    replica, side = place // 2, place % 2
    parity = replica % 2
    pairs = pair_order.shape[1] // 2
    quarter = row_count // 4
    local = jnp.arange(row_count, dtype=jnp.int32)
    block = local // quarter
    by_core = (block >> 1, block & 1)
    by_chip = (block & 1, block >> 1)
    examples = lax.dynamic_index_in_dim(row_example, replica, 1, keepdims=False)

    def onehots(order):
        other_core, other_chip = order
        example_of = (
            (side ^ other_core) * (2 * quarter) + (parity ^ other_chip) * quarter + local % quarter
        )
        return (examples[:, None, :] == example_of[None, :, None]).astype(jnp.bfloat16)

    onehot_core, onehot_chip = onehots(by_core), onehots(by_chip)

    def times_heads(rows):
        return jnp.dot(rows, head_weight, preferred_element_type=jnp.float32)

    logits = []
    for m in range(micro_count):
        rows = jnp.dot(onehot_core[m], states[m], preferred_element_type=jnp.float32)
        rows = rows.astype(jnp.bfloat16)
        far = swap(times_heads(rows[3 * quarter :]).astype(jnp.bfloat16), "rep", 1)
        home = swap(times_heads(rows[2 * quarter : 3 * quarter]).astype(jnp.bfloat16), "rep", 1)
        own = times_heads(rows[: 2 * quarter])
        far = (own[quarter:] + far.astype(jnp.float32)).astype(jnp.bfloat16)
        home = (own[:quarter] + home.astype(jnp.float32)).astype(jnp.bfloat16)
        logits.append((home, far))
    sib = swap(logits[0][1], "rep", 2)
    codes = routes(after(pair_order, *logits[-1]), head_weight.shape[1])
    chip_rows = jnp.einsum(
        "mei,miw->mew", onehot_chip, after(states, *logits[-1]), preferred_element_type=jnp.float32
    )
    chip_rows = chip_rows.astype(jnp.bfloat16)

    def settle(home, sib, first, second, to_home_first):
        grad_home = difference(home, jnp.where(to_home_first, first, second))
        grad_sib = difference(sib, jnp.where(to_home_first, second, first))
        return grad_home, grad_sib

    def leaving(home, sib, home_first):
        return jnp.where(home_first, home, sib), jnp.where(home_first, sib, home)

    def back(*blocks):
        gradient = jnp.concatenate(blocks, axis=0)
        partial = jnp.einsum(
            "rv,wv->rw", gradient, head_weight, preferred_element_type=jnp.float32
        )
        other = swap(partial.astype(jnp.bfloat16), "voc", 1)
        return (partial + other.astype(jnp.float32)).astype(jnp.bfloat16)

    def first_beside(nexts, settled):
        arriving = [swap(far, "rep", 2) for far in nexts]
        returned = [(swap(home, "rep", 1), swap(sib, "rep", 2)) for home, sib in settled]
        return arriving, returned

    def second_beside(returned):
        done = []
        for home, near, far in returned:
            farther = swap(far, "rep", 1)
            done.append((farther, back(home, near, far, farther)))
        return done

    grads, canon, settled = [], [], []
    for m in range(micro_count):
        home = logits[m][0]
        branches, (home_first, to_home_first) = codes[m]
        sent = leaving(home, sib, home_first)
        nexts = [] if m + 1 == micro_count else [logits[m + 1][1]]
        if settled:
            sent = [after(block, *settled[0]) for block in sent]
        first, (arriving, returned) = move_pairs(
            sent[0], branches[0], pairs, first_beside, nexts, settled
        )
        returned = [(group[0], *more) for group, more in zip(settled, returned)]
        second, done = move_pairs(
            after(sent[1], first), branches[1], pairs, second_beside, returned
        )
        for group, (farther, state) in zip(returned, done):
            grads += [*group, farther]
            canon.append(state)
        settled = [settle(home, sib, first, second, to_home_first)]
        sib = arriving[0] if arriving else None
    [(grad_home, grad_sib)] = settled
    far = swap(grad_sib, "rep", 2)
    near = swap(grad_home, "rep", 1)
    state_near = back(grad_home, near)
    far = after(far, state_near)
    farther = swap(far, "rep", 1)
    grads += [grad_home, near, far, farther]
    canon.append(jnp.concatenate([state_near, back(far, farther)], axis=0))
    state_grad = jnp.einsum(
        "mei,mew->miw", onehot_chip, jnp.stack(canon), preferred_element_type=jnp.float32
    ).astype(jnp.bfloat16)
    head_grad = head_gradient(
        chip_rows.reshape(micro_count * row_count, half_width), grads
    )
    return state_grad, head_grad


def spread_body(states, head_weight, pair_order, row_example):
    micro_count, row_count, half_width = states.shape
    devices = lax.axis_size("rep")
    place = lax.axis_index("rep")
    replica, side = place // 2, place % 2
    half = row_count // 2
    local = jnp.arange(row_count, dtype=jnp.int32)
    example_of = (side ^ (local // half)) * half + local % half
    examples = lax.dynamic_index_in_dim(row_example, replica, 1, keepdims=False)
    onehot = (examples[:, None, :] == example_of[None, :, None]).astype(jnp.bfloat16)
    ordered = jnp.einsum("mei,miw->mew", onehot, states, preferred_element_type=jnp.float32)
    ordered = ordered.astype(jnp.bfloat16)
    partner = partner_table(pair_order)
    sources = jnp.arange(devices, dtype=jnp.int32)
    partner_dev = 2 * jnp.repeat(partner, 2, axis=1) + sources % 2
    state_parts, gradients = [], []
    for m in range(micro_count):
        partial = jnp.dot(ordered[m], head_weight, preferred_element_type=jnp.float32)
        logits = (partial[:half] + swap(partial[half:], "rep", 1)).astype(jnp.bfloat16)
        tiles = logits.reshape(devices, half // devices, -1)
        tiles = lax.all_to_all(tiles, "rep", split_axis=0, concat_axis=0, tiled=True)
        mates = (partner_dev[m][:, None] == sources[None, :]).astype(jnp.bfloat16)
        mate_tiles = jnp.einsum("ds,srv->drv", mates, tiles, preferred_element_type=jnp.float32)
        graded = difference(tiles, mate_tiles)
        graded = lax.all_to_all(graded, "rep", split_axis=0, concat_axis=0, tiled=True)
        graded = graded.reshape(half, -1)
        gradient = jnp.concatenate([graded, swap(graded, "rep", 1)], axis=0)
        gradients.append(gradient)
        back = jnp.einsum("rv,wv->rw", gradient, head_weight, preferred_element_type=jnp.float32)
        state_canon = sum_over(back, "voc").astype(jnp.bfloat16)
        state_parts.append(
            jnp.einsum("ei,ew->iw", onehot[m], state_canon, preferred_element_type=jnp.float32)
        )
    state_grad = jnp.stack(state_parts).astype(jnp.bfloat16)
    head_grad = jnp.einsum(
        "mrw,mrv->wv", ordered, jnp.stack(gradients), preferred_element_type=jnp.float32
    )
    return state_grad, head_grad.astype(jnp.bfloat16)


def solution(mesh):
    replicas = mesh.shape["rep"] // 2
    few = replicas % 2 == 0 and math.factorial(replicas // 2) <= max_permutations
    few = few and mesh.shape["voc"] == 2
    return jax.shard_map(
        paired_body if few else spread_body,
        mesh=mesh,
        in_specs=(P(None, None, "rep"), P("rep", "voc"), P(), P()),
        out_specs=(P(None, None, "rep"), P("rep", "voc")),
        check_vma=False,
    )
```

```python
import functools
import itertools
import math

import jax
import jax.numpy as jnp
from jax import lax
from jax.experimental import pallas as pl
from jax.experimental.pallas import tpu as pltpu
from jax.sharding import PartitionSpec as P

distill_weight = 0.0625
max_permutations = 24
head_parts = 4


def partner_table(pair_order):
    slot_count = pair_order.shape[1]
    slot_ids = jnp.arange(slot_count, dtype=jnp.int32)
    matches = pair_order[:, None, :] == slot_ids[None, :, None]
    following = jnp.roll(pair_order, -1, axis=1)
    return jnp.sum(jnp.where(matches, following[:, None, :], 0), axis=2)


def route_kernel(order_ref, *refs):
    *branch_refs, flags_ref, dest, src, color = refs
    micro_count, replicas = order_ref.shape
    pairs = replicas // 2
    replica = lax.axis_index("rep") // 2
    for m in range(micro_count):
        for k in range(replicas):
            to, frm = order_ref[m, k], order_ref[m, (k + 1) % replicas]
            dest[frm] = to
            src[to] = frm
            color[k] = -1
        for start in range(0, replicas, 2):
            at = jnp.where(color[start] == 1, start + 1, start)
            for _ in range(pairs):
                color[at] = 0
                color[at ^ 1] = 1
                at = src[dest[at ^ 1] ^ 1]
        for c in range(2):
            sigma = []
            place = jnp.int32(0)
            for z in range(pairs):
                leaves = jnp.where(color[2 * z] == c, 2 * z, 2 * z + 1)
                to = dest[leaves] // 2
                smaller = to
                for earlier in sigma:
                    smaller = smaller - jnp.where(earlier < to, 1, 0)
                place = place * (pairs - z) + smaller
                sigma.append(to)
            branch_refs[2 * m + c][0] = place
        for row, moved in enumerate((replica, src[replica])):
            at = 2 * m + row
            flags_ref[at : at + 1, :] = jnp.full((1, flags_ref.shape[1]), color[moved], jnp.int32)


def routes(pair_order, width):
    micro_count, replicas = pair_order.shape
    smem = pl.BlockSpec(memory_space=pltpu.SMEM)
    *branches, flags = pl.pallas_call(
        route_kernel,
        out_shape=[jax.ShapeDtypeStruct((1,), jnp.int32)] * (2 * micro_count)
        + [jax.ShapeDtypeStruct((2 * micro_count, width), jnp.int32)],
        in_specs=[smem],
        out_specs=[smem] * (2 * micro_count) + [pl.BlockSpec(memory_space=pltpu.VMEM)],
        scratch_shapes=[pltpu.SMEM((replicas,), jnp.int32)] * 3,
        compiler_params=pltpu.CompilerParams(vmem_limit_bytes=1 << 20),
    )(pair_order)
    branch = [number.reshape(()) for number in branches]
    flag = [flags[at : at + 1] == 0 for at in range(2 * micro_count)]
    return [(branch[2 * m : 2 * m + 2], flag[2 * m : 2 * m + 2]) for m in range(micro_count)]


def move_pairs(block, branch, pairs, beside, *given):
    def one(sigma, moved, *rest):
        if any(z != to for z, to in enumerate(sigma)):
            route = [(z * 4 + low, to * 4 + low) for z, to in enumerate(sigma) for low in range(4)]
            moved = lax.ppermute(moved, "rep", route)
        return moved, beside(*rest)

    every = [functools.partial(one, sigma) for sigma in itertools.permutations(range(pairs))]
    return lax.switch(branch, every, block, *given)


def swap(block, axis, bit):
    count = lax.axis_size(axis)
    return lax.ppermute(block, axis, [(i, i ^ bit) for i in range(count)])


def difference(own, other):
    spread = own.astype(jnp.float32) - other.astype(jnp.float32)
    return (distill_weight * spread).astype(jnp.bfloat16)


def sum_over(block, axis):
    if lax.axis_size(axis) == 2:
        return block + swap(block, axis, 1)
    return lax.psum(block, axis)


def after(block, *others):
    return lax.optimization_barrier((block, *others))[0]


def head_kernel(*refs):
    rows_ref, *blocks, out_ref, whole, sums, in_sem, out_sem = refs
    height = blocks[0].shape[0]
    arriving = [
        pltpu.make_async_copy(block, whole.at[pl.ds(at * height, height)], in_sem.at[at])
        for at, block in enumerate(blocks)
    ]
    for copy in arriving:
        copy.start()
    for copy in arriving:
        copy.wait()
    step = whole.shape[1] // head_parts
    leaving = []
    for part in range(head_parts):
        columns = pl.ds(part * step, step)
        sums[:, columns] = lax.dot_general(
            rows_ref[...],
            whole[:, columns],
            (((0,), (0,)), ((), ())),
            preferred_element_type=jnp.float32,
        ).astype(sums.dtype)
        copy = pltpu.make_async_copy(sums.at[:, columns], out_ref.at[:, columns], out_sem.at[part])
        copy.start()
        leaving.append(copy)
    for copy in leaving:
        copy.wait()


def head_gradient(rows, blocks):
    count, width = rows.shape
    vocab = blocks[0].shape[1]
    anywhere = pl.BlockSpec(memory_space=pl.ANY)
    return pl.pallas_call(
        head_kernel,
        out_shape=jax.ShapeDtypeStruct((width, vocab), jnp.bfloat16),
        in_specs=[pl.BlockSpec(memory_space=pltpu.VMEM)] + [anywhere] * len(blocks),
        out_specs=anywhere,
        scratch_shapes=[
            pltpu.VMEM((count, vocab), jnp.bfloat16),
            pltpu.VMEM((width, vocab), jnp.bfloat16),
            pltpu.SemaphoreType.DMA((len(blocks),)),
            pltpu.SemaphoreType.DMA((head_parts,)),
        ],
        compiler_params=pltpu.CompilerParams(vmem_limit_bytes=24 << 20),
        cost_estimate=pl.CostEstimate(
            flops=2 * count * width * vocab,
            bytes_accessed=2 * (count * width + count * vocab + width * vocab),
            transcendentals=0,
        ),
    )(rows, *blocks)


def after(block, *others):
    return lax.optimization_barrier((block, *others))[0]


def head_kernel(*refs):
    rows_ref, *blocks, out_ref, whole = refs
    height = blocks[0].shape[0]
    for at, block in enumerate(blocks):
        whole[pl.ds(at * height, height), :] = block[...]
    out_ref[...] = lax.dot_general(
        rows_ref[...], whole[...], (((0,), (0,)), ((), ())), preferred_element_type=jnp.float32
    ).astype(out_ref.dtype)


def head_gradient(rows, blocks):
    count, width = rows.shape
    vocab = blocks[0].shape[1]
    return pl.pallas_call(
        head_kernel,
        out_shape=jax.ShapeDtypeStruct((width, vocab), jnp.bfloat16),
        scratch_shapes=[pltpu.VMEM((count, vocab), jnp.bfloat16)],
        compiler_params=pltpu.CompilerParams(vmem_limit_bytes=24 << 20),
        cost_estimate=pl.CostEstimate(
            flops=2 * count * width * vocab,
            bytes_accessed=2 * (count * width + count * vocab + width * vocab),
            transcendentals=0,
        ),
    )(rows, *blocks)


def after(block, *others):
    return lax.optimization_barrier((block, *others))[0]


def head_kernel(*refs):
    rows_ref, *blocks, out_ref, whole = refs
    height = blocks[0].shape[0]
    for at, block in enumerate(blocks):
        whole[pl.ds(at * height, height), :] = block[...]
    out_ref[...] = lax.dot_general(
        rows_ref[...], whole[...], (((0,), (0,)), ((), ())), preferred_element_type=jnp.float32
    ).astype(out_ref.dtype)


def head_gradient(rows, blocks):
    count, width = rows.shape
    height, vocab = blocks[0].shape
    step = vocab // 4
    return pl.pallas_call(
        head_kernel,
        grid=(vocab // step,),
        out_shape=jax.ShapeDtypeStruct((width, vocab), jnp.bfloat16),
        in_specs=[pl.BlockSpec((count, width), lambda i: (0, 0))]
        + [pl.BlockSpec((height, step), lambda i: (0, i))] * len(blocks),
        out_specs=pl.BlockSpec((width, step), lambda i: (0, i)),
        scratch_shapes=[pltpu.VMEM((count, step), jnp.bfloat16)],
        compiler_params=pltpu.CompilerParams(vmem_limit_bytes=16 << 20),
        cost_estimate=pl.CostEstimate(
            flops=2 * count * width * vocab,
            bytes_accessed=2 * (count * width + count * vocab + width * vocab),
            transcendentals=0,
        ),
    )(rows, *blocks)


def paired_body(states, head_weight, pair_order, row_example):
    micro_count, row_count, half_width = states.shape
    place = lax.axis_index("rep")
    replica, side = place // 2, place % 2
    parity = replica % 2
    pairs = pair_order.shape[1] // 2
    quarter = row_count // 4
    local = jnp.arange(row_count, dtype=jnp.int32)
    block = local // quarter
    by_core = (block >> 1, block & 1)
    by_chip = (block & 1, block >> 1)
    examples = lax.dynamic_index_in_dim(row_example, replica, 1, keepdims=False)

    def onehots(order):
        other_core, other_chip = order
        example_of = (
            (side ^ other_core) * (2 * quarter) + (parity ^ other_chip) * quarter + local % quarter
        )
        return (examples[:, None, :] == example_of[None, :, None]).astype(jnp.bfloat16)

    onehot_core, onehot_chip = onehots(by_core), onehots(by_chip)

    logits = []
    for m in range(micro_count):
        rows = jnp.dot(onehot_core[m], states[m], preferred_element_type=jnp.float32)
        rows = rows.astype(jnp.bfloat16)
        theirs = jnp.dot(rows[2 * quarter :], head_weight, preferred_element_type=jnp.float32)
        arrived = swap(theirs, "rep", 1)
        own = jnp.dot(rows[: 2 * quarter], head_weight, preferred_element_type=jnp.float32)
        far = (own[quarter:] + arrived[quarter:]).astype(jnp.bfloat16)
        home = (own[:quarter] + arrived[:quarter]).astype(jnp.bfloat16)
        logits.append((home, far))
    sib = swap(logits[0][1], "rep", 2)
    codes = routes(after(pair_order, *logits[-1]), head_weight.shape[1])
    chip_rows = jnp.einsum(
        "mei,miw->mew", onehot_chip, after(states, *logits[0]), preferred_element_type=jnp.float32
    )
    chip_rows = chip_rows.astype(jnp.bfloat16)

    def settle(home, sib, first, second, to_home_first):
        grad_home = difference(home, jnp.where(to_home_first, first, second))
        grad_sib = difference(sib, jnp.where(to_home_first, second, first))
        return grad_home, grad_sib

    def leaving(home, sib, home_first):
        return jnp.where(home_first, home, sib), jnp.where(home_first, sib, home)

    def partial_state(*blocks):
        gradient = jnp.concatenate(blocks, axis=0)
        partial = jnp.einsum(
            "rv,wv->rw", gradient, head_weight, preferred_element_type=jnp.float32
        )
        return partial, partial.astype(jnp.bfloat16)

    def whole_state(partial, sent, *before):
        other = after(swap(sent, "voc", 1), *before).astype(jnp.float32)
        return (partial + other).astype(jnp.bfloat16)

    def beside(nexts, settled):
        arriving = [swap(far, "rep", 2) for far in nexts]
        return arriving, [swap(grad_sib, "rep", 2) for _, grad_sib in settled]

    def second_beside(returned):
        return [(swap(home, "rep", 1), swap(far, "rep", 1)) for home, far in returned]

    early, settled = [], []
    for m in range(micro_count):
        home = logits[m][0]
        branches, (home_first, to_home_first) = codes[m]
        sent = leaving(home, sib, home_first)
        nexts = [] if m + 1 == micro_count else [logits[m + 1][1]]
        if m == 0:
            sent = [after(block, chip_rows) for block in sent]
        else:
            sent = [after(block, *settled[0]) for block in sent]
        first, (arriving, returned) = move_pairs(
            sent[0], branches[0], pairs, beside, nexts, settled
        )
        returned = [(group[0], far) for group, far in zip(settled, returned)]
        second, swapped = move_pairs(
            after(sent[1], first), branches[1], pairs, second_beside, returned
        )
        for (grad_home, far), (near, farther) in zip(returned, swapped):
            early.append((grad_home, near, far, farther))
        settled = [settle(home, sib, first, second, to_home_first)]
        sib = arriving[0] if arriving else None
    [(grad_home, grad_sib)] = settled
    far = swap(grad_sib, "rep", 2)
    near = swap(grad_home, "rep", 1)
    early = [[after(block, near) for block in group] for group in early]
    parts = [partial_state(*group) for group in [*early, (grad_home, near)]]
    far = after(far, *[sent for _, sent in parts])
    farther = swap(far, "rep", 1)
    head_grad = head_gradient(
        chip_rows.reshape(micro_count * row_count, half_width),
        sum(early, []) + [grad_home, near, far, farther],
    )
    canon = [whole_state(*part, head_grad) for part in parts[:-1]]
    last = [whole_state(*parts[-1]), whole_state(*partial_state(far, farther))]
    canon.append(jnp.concatenate(last, axis=0))
    state_grad = jnp.einsum(
        "mei,mew->miw", onehot_chip, jnp.stack(canon), preferred_element_type=jnp.float32
    ).astype(jnp.bfloat16)
    return state_grad, head_grad


def spread_body(states, head_weight, pair_order, row_example):
    micro_count, row_count, half_width = states.shape
    devices = lax.axis_size("rep")
    place = lax.axis_index("rep")
    replica, side = place // 2, place % 2
    half = row_count // 2
    local = jnp.arange(row_count, dtype=jnp.int32)
    example_of = (side ^ (local // half)) * half + local % half
    examples = lax.dynamic_index_in_dim(row_example, replica, 1, keepdims=False)
    onehot = (examples[:, None, :] == example_of[None, :, None]).astype(jnp.bfloat16)
    ordered = jnp.einsum("mei,miw->mew", onehot, states, preferred_element_type=jnp.float32)
    ordered = ordered.astype(jnp.bfloat16)
    partner = partner_table(pair_order)
    sources = jnp.arange(devices, dtype=jnp.int32)
    partner_dev = 2 * jnp.repeat(partner, 2, axis=1) + sources % 2
    state_parts, gradients = [], []
    for m in range(micro_count):
        partial = jnp.dot(ordered[m], head_weight, preferred_element_type=jnp.float32)
        logits = (partial[:half] + swap(partial[half:], "rep", 1)).astype(jnp.bfloat16)
        tiles = logits.reshape(devices, half // devices, -1)
        tiles = lax.all_to_all(tiles, "rep", split_axis=0, concat_axis=0, tiled=True)
        mates = (partner_dev[m][:, None] == sources[None, :]).astype(jnp.bfloat16)
        mate_tiles = jnp.einsum("ds,srv->drv", mates, tiles, preferred_element_type=jnp.float32)
        graded = difference(tiles, mate_tiles)
        graded = lax.all_to_all(graded, "rep", split_axis=0, concat_axis=0, tiled=True)
        graded = graded.reshape(half, -1)
        gradient = jnp.concatenate([graded, swap(graded, "rep", 1)], axis=0)
        gradients.append(gradient)
        back = jnp.einsum("rv,wv->rw", gradient, head_weight, preferred_element_type=jnp.float32)
        state_canon = sum_over(back, "voc").astype(jnp.bfloat16)
        state_parts.append(
            jnp.einsum("ei,ew->iw", onehot[m], state_canon, preferred_element_type=jnp.float32)
        )
    state_grad = jnp.stack(state_parts).astype(jnp.bfloat16)
    head_grad = jnp.einsum(
        "mrw,mrv->wv", ordered, jnp.stack(gradients), preferred_element_type=jnp.float32
    )
    return state_grad, head_grad.astype(jnp.bfloat16)


def solution(mesh):
    replicas = mesh.shape["rep"] // 2
    few = replicas % 2 == 0 and math.factorial(replicas // 2) <= max_permutations
    few = few and mesh.shape["voc"] == 2
    return jax.shard_map(
        paired_body if few else spread_body,
        mesh=mesh,
        in_specs=(P(None, None, "rep"), P("rep", "voc"), P(), P()),
        out_specs=(P(None, None, "rep"), P("rep", "voc")),
        check_vma=False,
    )
```

```python
import functools
import itertools
import math

import jax
import jax.numpy as jnp
from jax import lax
from jax.experimental import pallas as pl
from jax.experimental.pallas import tpu as pltpu
from jax.sharding import PartitionSpec as P

distill_weight = 0.0625
max_permutations = 24
head_parts = 4


def partner_table(pair_order):
    slot_count = pair_order.shape[1]
    slot_ids = jnp.arange(slot_count, dtype=jnp.int32)
    matches = pair_order[:, None, :] == slot_ids[None, :, None]
    following = jnp.roll(pair_order, -1, axis=1)
    return jnp.sum(jnp.where(matches, following[:, None, :], 0), axis=2)


def route_kernel(order_ref, *refs):
    *branch_refs, flags_ref, dest, src, color = refs
    micro_count, replicas = order_ref.shape
    pairs = replicas // 2
    replica = lax.axis_index("rep") // 2
    for m in range(micro_count):
        for k in range(replicas):
            to, frm = order_ref[m, k], order_ref[m, (k + 1) % replicas]
            dest[frm] = to
            src[to] = frm
            color[k] = -1
        for start in range(0, replicas, 2):
            at = jnp.where(color[start] == 1, start + 1, start)
            for _ in range(pairs):
                color[at] = 0
                color[at ^ 1] = 1
                at = src[dest[at ^ 1] ^ 1]
        for c in range(2):
            sigma = []
            place = jnp.int32(0)
            for z in range(pairs):
                leaves = jnp.where(color[2 * z] == c, 2 * z, 2 * z + 1)
                to = dest[leaves] // 2
                smaller = to
                for earlier in sigma:
                    smaller = smaller - jnp.where(earlier < to, 1, 0)
                place = place * (pairs - z) + smaller
                sigma.append(to)
            branch_refs[2 * m + c][0] = place
        for row, moved in enumerate((replica, src[replica])):
            at = 2 * m + row
            flags_ref[at : at + 1, :] = jnp.full((1, flags_ref.shape[1]), color[moved], jnp.int32)


def routes(pair_order, width):
    micro_count, replicas = pair_order.shape
    smem = pl.BlockSpec(memory_space=pltpu.SMEM)
    *branches, flags = pl.pallas_call(
        route_kernel,
        out_shape=[jax.ShapeDtypeStruct((1,), jnp.int32)] * (2 * micro_count)
        + [jax.ShapeDtypeStruct((2 * micro_count, width), jnp.int32)],
        in_specs=[smem],
        out_specs=[smem] * (2 * micro_count) + [pl.BlockSpec(memory_space=pltpu.VMEM)],
        scratch_shapes=[pltpu.SMEM((replicas,), jnp.int32)] * 3,
        compiler_params=pltpu.CompilerParams(vmem_limit_bytes=1 << 20),
    )(pair_order)
    branch = [number.reshape(()) for number in branches]
    flag = [flags[at : at + 1] == 0 for at in range(2 * micro_count)]
    return [(branch[2 * m : 2 * m + 2], flag[2 * m : 2 * m + 2]) for m in range(micro_count)]


def move_pairs(block, branch, pairs, beside, *given):
    def one(sigma, moved, *rest):
        if any(z != to for z, to in enumerate(sigma)):
            route = [(z * 4 + low, to * 4 + low) for z, to in enumerate(sigma) for low in range(4)]
            moved = lax.ppermute(moved, "rep", route)
        return moved, beside(*rest)

    every = [functools.partial(one, sigma) for sigma in itertools.permutations(range(pairs))]
    return lax.switch(branch, every, block, *given)


def swap(block, axis, bit):
    count = lax.axis_size(axis)
    return lax.ppermute(block, axis, [(i, i ^ bit) for i in range(count)])


def difference(own, other):
    spread = own.astype(jnp.float32) - other.astype(jnp.float32)
    return (distill_weight * spread).astype(jnp.bfloat16)


def sum_over(block, axis):
    if lax.axis_size(axis) == 2:
        return block + swap(block, axis, 1)
    return lax.psum(block, axis)


def after(block, *others):
    return lax.optimization_barrier((block, *others))[0]


def head_kernel(*refs):
    rows_ref, *blocks, out_ref, whole, sums, in_sem, out_sem = refs
    height = blocks[0].shape[0]
    arriving = [
        pltpu.make_async_copy(block, whole.at[pl.ds(at * height, height)], in_sem.at[at])
        for at, block in enumerate(blocks)
    ]
    for copy in arriving:
        copy.start()
    for copy in arriving:
        copy.wait()
    step = whole.shape[1] // head_parts
    leaving = []
    for part in range(head_parts):
        columns = pl.ds(part * step, step)
        sums[:, columns] = lax.dot_general(
            rows_ref[...],
            whole[:, columns],
            (((0,), (0,)), ((), ())),
            preferred_element_type=jnp.float32,
        ).astype(sums.dtype)
        copy = pltpu.make_async_copy(sums.at[:, columns], out_ref.at[:, columns], out_sem.at[part])
        copy.start()
        leaving.append(copy)
    for copy in leaving:
        copy.wait()


def head_gradient(rows, blocks):
    count, width = rows.shape
    vocab = blocks[0].shape[1]
    anywhere = pl.BlockSpec(memory_space=pl.ANY)
    return pl.pallas_call(
        head_kernel,
        out_shape=jax.ShapeDtypeStruct((width, vocab), jnp.bfloat16),
        in_specs=[pl.BlockSpec(memory_space=pltpu.VMEM)] + [anywhere] * len(blocks),
        out_specs=anywhere,
        scratch_shapes=[
            pltpu.VMEM((count, vocab), jnp.bfloat16),
            pltpu.VMEM((width, vocab), jnp.bfloat16),
            pltpu.SemaphoreType.DMA((len(blocks),)),
            pltpu.SemaphoreType.DMA((head_parts,)),
        ],
        compiler_params=pltpu.CompilerParams(vmem_limit_bytes=24 << 20),
        cost_estimate=pl.CostEstimate(
            flops=2 * count * width * vocab,
            bytes_accessed=2 * (count * width + count * vocab + width * vocab),
            transcendentals=0,
        ),
    )(rows, *blocks)


def after(block, *others):
    return lax.optimization_barrier((block, *others))[0]


def head_kernel(*refs):
    rows_ref, *blocks, out_ref, whole = refs
    height = blocks[0].shape[0]
    for at, block in enumerate(blocks):
        whole[pl.ds(at * height, height), :] = block[...]
    out_ref[...] = lax.dot_general(
        rows_ref[...], whole[...], (((0,), (0,)), ((), ())), preferred_element_type=jnp.float32
    ).astype(out_ref.dtype)


def head_gradient(rows, blocks):
    count, width = rows.shape
    vocab = blocks[0].shape[1]
    return pl.pallas_call(
        head_kernel,
        out_shape=jax.ShapeDtypeStruct((width, vocab), jnp.bfloat16),
        scratch_shapes=[pltpu.VMEM((count, vocab), jnp.bfloat16)],
        compiler_params=pltpu.CompilerParams(vmem_limit_bytes=24 << 20),
        cost_estimate=pl.CostEstimate(
            flops=2 * count * width * vocab,
            bytes_accessed=2 * (count * width + count * vocab + width * vocab),
            transcendentals=0,
        ),
    )(rows, *blocks)


def after(block, *others):
    return lax.optimization_barrier((block, *others))[0]


def head_kernel(*refs):
    rows_ref, *blocks, out_ref, whole = refs
    height = blocks[0].shape[0]
    for at, block in enumerate(blocks):
        whole[pl.ds(at * height, height), :] = block[...]
    out_ref[...] = lax.dot_general(
        rows_ref[...], whole[...], (((0,), (0,)), ((), ())), preferred_element_type=jnp.float32
    ).astype(out_ref.dtype)


def head_gradient(rows, blocks):
    count, width = rows.shape
    height, vocab = blocks[0].shape
    step = vocab // 4
    return pl.pallas_call(
        head_kernel,
        grid=(vocab // step,),
        out_shape=jax.ShapeDtypeStruct((width, vocab), jnp.bfloat16),
        in_specs=[pl.BlockSpec((count, width), lambda i: (0, 0))]
        + [pl.BlockSpec((height, step), lambda i: (0, i))] * len(blocks),
        out_specs=pl.BlockSpec((width, step), lambda i: (0, i)),
        scratch_shapes=[pltpu.VMEM((count, step), jnp.bfloat16)],
        compiler_params=pltpu.CompilerParams(vmem_limit_bytes=16 << 20),
        cost_estimate=pl.CostEstimate(
            flops=2 * count * width * vocab,
            bytes_accessed=2 * (count * width + count * vocab + width * vocab),
            transcendentals=0,
        ),
    )(rows, *blocks)


def paired_body(states, head_weight, pair_order, row_example):
    micro_count, row_count, half_width = states.shape
    place = lax.axis_index("rep")
    replica, side = place // 2, place % 2
    parity = replica % 2
    pairs = pair_order.shape[1] // 2
    quarter = row_count // 4
    local = jnp.arange(row_count, dtype=jnp.int32)
    block = local // quarter
    by_core = (block >> 1, block & 1)
    by_chip = (block & 1, block >> 1)
    examples = lax.dynamic_index_in_dim(row_example, replica, 1, keepdims=False)

    def onehots(order):
        other_core, other_chip = order
        example_of = (
            (side ^ other_core) * (2 * quarter) + (parity ^ other_chip) * quarter + local % quarter
        )
        return (examples[:, None, :] == example_of[None, :, None]).astype(jnp.bfloat16)

    onehot_core, onehot_chip = onehots(by_core), onehots(by_chip)

    logits = []
    for m in range(micro_count):
        rows = jnp.dot(onehot_core[m], states[m], preferred_element_type=jnp.float32)
        rows = rows.astype(jnp.bfloat16)
        theirs = jnp.dot(rows[2 * quarter :], head_weight, preferred_element_type=jnp.float32)
        arrived = swap(theirs, "rep", 1)
        own = jnp.dot(rows[: 2 * quarter], head_weight, preferred_element_type=jnp.float32)
        far = (own[quarter:] + arrived[quarter:]).astype(jnp.bfloat16)
        home = (own[:quarter] + arrived[:quarter]).astype(jnp.bfloat16)
        logits.append((home, far))
    sib = swap(logits[0][1], "rep", 2)
    codes = routes(after(pair_order, *logits[-1]), head_weight.shape[1])
    def settle(home, sib, first, second, to_home_first):
        grad_home = difference(home, jnp.where(to_home_first, first, second))
        grad_sib = difference(sib, jnp.where(to_home_first, second, first))
        return grad_home, grad_sib

    def leaving(home, sib, home_first):
        return jnp.where(home_first, home, sib), jnp.where(home_first, sib, home)

    def partial_state(heads, *blocks):
        gradient = jnp.concatenate(blocks, axis=0)
        partial = jnp.einsum("rv,wv->rw", gradient, heads, preferred_element_type=jnp.float32)
        return partial, partial.astype(jnp.bfloat16)

    def beside(nexts, settled):
        arriving = [swap(far, "rep", 2) for far in nexts]
        return arriving, [swap(grad_sib, "rep", 2) for _, grad_sib in settled]

    def second_beside(returned):
        return [(swap(home, "rep", 1), swap(far, "rep", 1)) for home, far in returned]

    early, settled = [], []
    for m in range(micro_count):
        home = logits[m][0]
        branches, (home_first, to_home_first) = codes[m]
        sent = leaving(home, sib, home_first)
        nexts = [] if m + 1 == micro_count else [logits[m + 1][1]]
        if m > 0:
            sent = [after(block, *settled[0]) for block in sent]
        first, (arriving, returned) = move_pairs(
            sent[0], branches[0], pairs, beside, nexts, settled
        )
        returned = [(group[0], far) for group, far in zip(settled, returned)]
        second, swapped = move_pairs(
            after(sent[1], first), branches[1], pairs, second_beside, returned
        )
        for (grad_home, far), (near, farther) in zip(returned, swapped):
            early.append((grad_home, near, far, farther))
        settled = [settle(home, sib, first, second, to_home_first)]
        sib = arriving[0] if arriving else None
    [(grad_home, grad_sib)] = settled
    far = swap(grad_sib, "rep", 2)
    near = swap(grad_home, "rep", 1)
    heads = after(head_weight, grad_sib)
    early = [[after(block, near) for block in group] for group in early]
    chip_rows = jnp.einsum(
        "mei,miw->mew", onehot_chip, after(states, near), preferred_element_type=jnp.float32
    )
    chip_rows = chip_rows.astype(jnp.bfloat16)
    parts = [partial_state(heads, *group) for group in early]
    early_other = [swap(sent, "voc", 1) for _, sent in parts]
    near_part = partial_state(heads, grad_home, near)
    far = after(far, near_part[1], *early_other)
    farther = swap(far, "rep", 1)
    far_part = partial_state(heads, far, farther)
    head_grad = head_gradient(
        chip_rows.reshape(micro_count * row_count, half_width),
        sum(early, []) + [grad_home, near, far, farther],
    )

    def whole_state(partial, other):
        return (partial + other.astype(jnp.float32)).astype(jnp.bfloat16)

    canon = [whole_state(part[0], other) for part, other in zip(parts, early_other)]
    last = [whole_state(part[0], swap(part[1], "voc", 1)) for part in (near_part, far_part)]
    canon.append(jnp.concatenate(last, axis=0))
    state_grad = jnp.einsum(
        "mei,mew->miw", onehot_chip, jnp.stack(canon), preferred_element_type=jnp.float32
    ).astype(jnp.bfloat16)
    return state_grad, head_grad


def spread_body(states, head_weight, pair_order, row_example):
    micro_count, row_count, half_width = states.shape
    devices = lax.axis_size("rep")
    place = lax.axis_index("rep")
    replica, side = place // 2, place % 2
    half = row_count // 2
    local = jnp.arange(row_count, dtype=jnp.int32)
    example_of = (side ^ (local // half)) * half + local % half
    examples = lax.dynamic_index_in_dim(row_example, replica, 1, keepdims=False)
    onehot = (examples[:, None, :] == example_of[None, :, None]).astype(jnp.bfloat16)
    ordered = jnp.einsum("mei,miw->mew", onehot, states, preferred_element_type=jnp.float32)
    ordered = ordered.astype(jnp.bfloat16)
    partner = partner_table(pair_order)
    sources = jnp.arange(devices, dtype=jnp.int32)
    partner_dev = 2 * jnp.repeat(partner, 2, axis=1) + sources % 2
    state_parts, gradients = [], []
    for m in range(micro_count):
        partial = jnp.dot(ordered[m], head_weight, preferred_element_type=jnp.float32)
        logits = (partial[:half] + swap(partial[half:], "rep", 1)).astype(jnp.bfloat16)
        tiles = logits.reshape(devices, half // devices, -1)
        tiles = lax.all_to_all(tiles, "rep", split_axis=0, concat_axis=0, tiled=True)
        mates = (partner_dev[m][:, None] == sources[None, :]).astype(jnp.bfloat16)
        mate_tiles = jnp.einsum("ds,srv->drv", mates, tiles, preferred_element_type=jnp.float32)
        graded = difference(tiles, mate_tiles)
        graded = lax.all_to_all(graded, "rep", split_axis=0, concat_axis=0, tiled=True)
        graded = graded.reshape(half, -1)
        gradient = jnp.concatenate([graded, swap(graded, "rep", 1)], axis=0)
        gradients.append(gradient)
        back = jnp.einsum("rv,wv->rw", gradient, head_weight, preferred_element_type=jnp.float32)
        state_canon = sum_over(back, "voc").astype(jnp.bfloat16)
        state_parts.append(
            jnp.einsum("ei,ew->iw", onehot[m], state_canon, preferred_element_type=jnp.float32)
        )
    state_grad = jnp.stack(state_parts).astype(jnp.bfloat16)
    head_grad = jnp.einsum(
        "mrw,mrv->wv", ordered, jnp.stack(gradients), preferred_element_type=jnp.float32
    )
    return state_grad, head_grad.astype(jnp.bfloat16)


def solution(mesh):
    replicas = mesh.shape["rep"] // 2
    few = replicas % 2 == 0 and math.factorial(replicas // 2) <= max_permutations
    few = few and mesh.shape["voc"] == 2
    return jax.shard_map(
        paired_body if few else spread_body,
        mesh=mesh,
        in_specs=(P(None, None, "rep"), P("rep", "voc"), P(), P()),
        out_specs=(P(None, None, "rep"), P("rep", "voc")),
        check_vma=False,
    )
```

```python
import functools
import itertools
import math

import jax
import jax.numpy as jnp
from jax import lax
from jax.experimental import pallas as pl
from jax.experimental.pallas import tpu as pltpu
from jax.sharding import PartitionSpec as P

distill_weight = 0.0625
max_permutations = 24
head_parts = 2


def partner_table(pair_order):
    slot_count = pair_order.shape[1]
    slot_ids = jnp.arange(slot_count, dtype=jnp.int32)
    matches = pair_order[:, None, :] == slot_ids[None, :, None]
    following = jnp.roll(pair_order, -1, axis=1)
    return jnp.sum(jnp.where(matches, following[:, None, :], 0), axis=2)


def route_kernel(order_ref, *refs):
    *branch_refs, flags_ref, dest, src, color = refs
    micro_count, replicas = order_ref.shape
    pairs = replicas // 2
    replica = lax.axis_index("rep") // 2
    for m in range(micro_count):
        for k in range(replicas):
            to, frm = order_ref[m, k], order_ref[m, (k + 1) % replicas]
            dest[frm] = to
            src[to] = frm
            color[k] = -1
        for start in range(0, replicas, 2):
            at = jnp.where(color[start] == 1, start + 1, start)
            for _ in range(pairs):
                color[at] = 0
                color[at ^ 1] = 1
                at = src[dest[at ^ 1] ^ 1]
        for c in range(2):
            sigma = []
            place = jnp.int32(0)
            for z in range(pairs):
                leaves = jnp.where(color[2 * z] == c, 2 * z, 2 * z + 1)
                to = dest[leaves] // 2
                smaller = to
                for earlier in sigma:
                    smaller = smaller - jnp.where(earlier < to, 1, 0)
                place = place * (pairs - z) + smaller
                sigma.append(to)
            branch_refs[2 * m + c][0] = place
        for row, moved in enumerate((replica, src[replica])):
            at = 2 * m + row
            flags_ref[at : at + 1, :] = jnp.full((1, flags_ref.shape[1]), color[moved], jnp.int32)


def routes(pair_order, width):
    micro_count, replicas = pair_order.shape
    smem = pl.BlockSpec(memory_space=pltpu.SMEM)
    *branches, flags = pl.pallas_call(
        route_kernel,
        out_shape=[jax.ShapeDtypeStruct((1,), jnp.int32)] * (2 * micro_count)
        + [jax.ShapeDtypeStruct((2 * micro_count, width), jnp.int32)],
        in_specs=[smem],
        out_specs=[smem] * (2 * micro_count) + [pl.BlockSpec(memory_space=pltpu.VMEM)],
        scratch_shapes=[pltpu.SMEM((replicas,), jnp.int32)] * 3,
        compiler_params=pltpu.CompilerParams(vmem_limit_bytes=1 << 20),
    )(pair_order)
    branch = [number.reshape(()) for number in branches]
    flag = [flags[at : at + 1] == 0 for at in range(2 * micro_count)]
    return [(branch[2 * m : 2 * m + 2], flag[2 * m : 2 * m + 2]) for m in range(micro_count)]


def move_pairs(block, branch, pairs, beside, *given):
    def one(sigma, moved, *rest):
        if any(z != to for z, to in enumerate(sigma)):
            route = [(z * 4 + low, to * 4 + low) for z, to in enumerate(sigma) for low in range(4)]
            moved = lax.ppermute(moved, "rep", route)
        return moved, beside(*rest)

    every = [functools.partial(one, sigma) for sigma in itertools.permutations(range(pairs))]
    return lax.switch(branch, every, block, *given)


def swap(block, axis, bit):
    count = lax.axis_size(axis)
    return lax.ppermute(block, axis, [(i, i ^ bit) for i in range(count)])


def difference(own, other):
    spread = own.astype(jnp.float32) - other.astype(jnp.float32)
    return (distill_weight * spread).astype(jnp.bfloat16)


def sum_over(block, axis):
    if lax.axis_size(axis) == 2:
        return block + swap(block, axis, 1)
    return lax.psum(block, axis)


def after(block, *others):
    return lax.optimization_barrier((block, *others))[0]


def head_kernel(*refs):
    rows_ref, *blocks, out_ref, whole, sums, in_sem, out_sem = refs
    height = blocks[0].shape[0]
    step = whole.shape[1] // head_parts
    arriving = []
    for part in range(head_parts):
        columns = pl.ds(part * step, step)
        for at, block in enumerate(blocks):
            copy = pltpu.make_async_copy(
                block.at[:, columns],
                whole.at[pl.ds(at * height, height), columns],
                in_sem.at[part, at],
            )
            copy.start()
            arriving.append(copy)
    leaving = []
    for part in range(head_parts):
        columns = pl.ds(part * step, step)
        for copy in arriving[part * len(blocks) : (part + 1) * len(blocks)]:
            copy.wait()
        sums[:, columns] = lax.dot_general(
            rows_ref[...],
            whole[:, columns],
            (((0,), (0,)), ((), ())),
            preferred_element_type=jnp.float32,
        ).astype(sums.dtype)
        copy = pltpu.make_async_copy(sums.at[:, columns], out_ref.at[:, columns], out_sem.at[part])
        copy.start()
        leaving.append(copy)
    for copy in leaving:
        copy.wait()


def head_gradient(rows, blocks):
    count, width = rows.shape
    vocab = blocks[0].shape[1]
    anywhere = pl.BlockSpec(memory_space=pl.ANY)
    return pl.pallas_call(
        head_kernel,
        out_shape=jax.ShapeDtypeStruct((width, vocab), jnp.bfloat16),
        in_specs=[pl.BlockSpec(memory_space=pltpu.VMEM)] + [anywhere] * len(blocks),
        out_specs=anywhere,
        scratch_shapes=[
            pltpu.VMEM((count, vocab), jnp.bfloat16),
            pltpu.VMEM((width, vocab), jnp.bfloat16),
            pltpu.SemaphoreType.DMA((head_parts, len(blocks))),
            pltpu.SemaphoreType.DMA((head_parts,)),
        ],
        compiler_params=pltpu.CompilerParams(vmem_limit_bytes=24 << 20),
        cost_estimate=pl.CostEstimate(
            flops=2 * count * width * vocab,
            bytes_accessed=2 * (count * width + count * vocab + width * vocab),
            transcendentals=0,
        ),
    )(rows, *blocks)


def after(block, *others):
    return lax.optimization_barrier((block, *others))[0]


def head_kernel(*refs):
    rows_ref, *blocks, out_ref, whole = refs
    height = blocks[0].shape[0]
    for at, block in enumerate(blocks):
        whole[pl.ds(at * height, height), :] = block[...]
    out_ref[...] = lax.dot_general(
        rows_ref[...], whole[...], (((0,), (0,)), ((), ())), preferred_element_type=jnp.float32
    ).astype(out_ref.dtype)


def head_gradient(rows, blocks):
    count, width = rows.shape
    vocab = blocks[0].shape[1]
    return pl.pallas_call(
        head_kernel,
        out_shape=jax.ShapeDtypeStruct((width, vocab), jnp.bfloat16),
        scratch_shapes=[pltpu.VMEM((count, vocab), jnp.bfloat16)],
        compiler_params=pltpu.CompilerParams(vmem_limit_bytes=24 << 20),
        cost_estimate=pl.CostEstimate(
            flops=2 * count * width * vocab,
            bytes_accessed=2 * (count * width + count * vocab + width * vocab),
            transcendentals=0,
        ),
    )(rows, *blocks)


def after(block, *others):
    return lax.optimization_barrier((block, *others))[0]


def head_kernel(*refs):
    rows_ref, *blocks, out_ref, whole = refs
    height = blocks[0].shape[0]
    for at, block in enumerate(blocks):
        whole[pl.ds(at * height, height), :] = block[...]
    out_ref[...] = lax.dot_general(
        rows_ref[...], whole[...], (((0,), (0,)), ((), ())), preferred_element_type=jnp.float32
    ).astype(out_ref.dtype)


def head_gradient(rows, blocks):
    count, width = rows.shape
    height, vocab = blocks[0].shape
    step = vocab // 4
    return pl.pallas_call(
        head_kernel,
        grid=(vocab // step,),
        out_shape=jax.ShapeDtypeStruct((width, vocab), jnp.bfloat16),
        in_specs=[pl.BlockSpec((count, width), lambda i: (0, 0))]
        + [pl.BlockSpec((height, step), lambda i: (0, i))] * len(blocks),
        out_specs=pl.BlockSpec((width, step), lambda i: (0, i)),
        scratch_shapes=[pltpu.VMEM((count, step), jnp.bfloat16)],
        compiler_params=pltpu.CompilerParams(vmem_limit_bytes=16 << 20),
        cost_estimate=pl.CostEstimate(
            flops=2 * count * width * vocab,
            bytes_accessed=2 * (count * width + count * vocab + width * vocab),
            transcendentals=0,
        ),
    )(rows, *blocks)


def paired_body(states, head_weight, pair_order, row_example):
    micro_count, row_count, half_width = states.shape
    place = lax.axis_index("rep")
    replica, side = place // 2, place % 2
    parity = replica % 2
    pairs = pair_order.shape[1] // 2
    quarter = row_count // 4
    local = jnp.arange(row_count, dtype=jnp.int32)
    block = local // quarter
    by_core = (block >> 1, block & 1)
    by_chip = (block & 1, block >> 1)
    examples = lax.dynamic_index_in_dim(row_example, replica, 1, keepdims=False)

    def onehots(order):
        other_core, other_chip = order
        example_of = (
            (side ^ other_core) * (2 * quarter) + (parity ^ other_chip) * quarter + local % quarter
        )
        return (examples[:, None, :] == example_of[None, :, None]).astype(jnp.bfloat16)

    onehot_core, onehot_chip = onehots(by_core), onehots(by_chip)

    logits = []
    for m in range(micro_count):
        rows = jnp.dot(onehot_core[m], states[m], preferred_element_type=jnp.float32)
        rows = rows.astype(jnp.bfloat16)
        theirs = jnp.dot(rows[2 * quarter :], head_weight, preferred_element_type=jnp.float32)
        arrived = swap(theirs, "rep", 1)
        own = jnp.dot(rows[: 2 * quarter], head_weight, preferred_element_type=jnp.float32)
        far = (own[quarter:] + arrived[quarter:]).astype(jnp.bfloat16)
        home = (own[:quarter] + arrived[:quarter]).astype(jnp.bfloat16)
        logits.append((home, far))
    sib = swap(logits[0][1], "rep", 2)
    codes = routes(after(pair_order, *logits[-1]), head_weight.shape[1])
    def settle(sent, arrived, home_first, to_home_first):
        home, sib = leaving(*sent, home_first)
        for_home, for_sib = leaving(*arrived, to_home_first)
        return difference(home, for_home), difference(sib, for_sib)

    def leaving(home, sib, home_first):
        return jnp.where(home_first, home, sib), jnp.where(home_first, sib, home)

    def partial_state(heads, *blocks):
        gradient = jnp.concatenate(blocks, axis=0)
        partial = jnp.einsum("rv,wv->rw", gradient, heads, preferred_element_type=jnp.float32)
        return partial, partial.astype(jnp.bfloat16)

    def beside(nexts, settled):
        arriving = [swap(far, "rep", 2) for far in nexts]
        return arriving, [swap(grad_sib, "rep", 2) for _, grad_sib in settled]

    def second_beside(returned):
        return [(swap(home, "rep", 1), swap(far, "rep", 1)) for home, far in returned]

    early, settled = [], []
    for m in range(micro_count):
        tiles = [logits[m][0], sib]
        branches, (home_first, to_home_first) = codes[m]
        nexts = [] if m + 1 == micro_count else [logits[m + 1][1]]
        if settled:
            tiles = [after(tile, *settled[0]) for tile in tiles]
        sent = leaving(*tiles, home_first)
        first, (arriving, returned) = move_pairs(
            sent[0], branches[0], pairs, beside, nexts, settled
        )
        returned = [(group[0], far) for group, far in zip(settled, returned)]
        second, swapped = move_pairs(
            after(sent[1], first), branches[1], pairs, second_beside, returned
        )
        for (grad_home, far), (near, farther) in zip(returned, swapped):
            early.append((grad_home, near, far, farther))
        settled = [settle(sent, (first, second), home_first, to_home_first)]
        sib = arriving[0] if arriving else None
    [(grad_home, grad_sib)] = settled
    far = swap(grad_sib, "rep", 2)
    near = swap(grad_home, "rep", 1)
    heads = after(head_weight, grad_sib)
    early = [[after(block, near) for block in group] for group in early]
    chip_rows = jnp.einsum(
        "mei,miw->mew", onehot_chip, after(states, near), preferred_element_type=jnp.float32
    )
    chip_rows = chip_rows.astype(jnp.bfloat16)
    parts = [partial_state(heads, *group) for group in early]
    early_other = [swap(sent, "voc", 1) for _, sent in parts]
    near_part = partial_state(heads, grad_home, near)
    far = after(far, near_part[1], *early_other)
    farther = swap(far, "rep", 1)
    far_part = partial_state(heads, far, farther)
    head_grad = head_gradient(
        chip_rows.reshape(micro_count * row_count, half_width),
        sum(early, []) + [grad_home, near, far, farther],
    )

    def whole_state(partial, other):
        return (partial + other.astype(jnp.float32)).astype(jnp.bfloat16)

    canon = [whole_state(part[0], other) for part, other in zip(parts, early_other)]
    near_other = after(swap(after(near_part[1], *early_other), "voc", 1), head_grad)
    last = [
        whole_state(near_part[0], near_other),
        whole_state(far_part[0], swap(far_part[1], "voc", 1)),
    ]
    canon.append(jnp.concatenate(last, axis=0))
    state_grad = jnp.einsum(
        "mei,mew->miw", onehot_chip, jnp.stack(canon), preferred_element_type=jnp.float32
    ).astype(jnp.bfloat16)
    return state_grad, head_grad


def spread_body(states, head_weight, pair_order, row_example):
    micro_count, row_count, half_width = states.shape
    devices = lax.axis_size("rep")
    place = lax.axis_index("rep")
    replica, side = place // 2, place % 2
    half = row_count // 2
    local = jnp.arange(row_count, dtype=jnp.int32)
    example_of = (side ^ (local // half)) * half + local % half
    examples = lax.dynamic_index_in_dim(row_example, replica, 1, keepdims=False)
    onehot = (examples[:, None, :] == example_of[None, :, None]).astype(jnp.bfloat16)
    ordered = jnp.einsum("mei,miw->mew", onehot, states, preferred_element_type=jnp.float32)
    ordered = ordered.astype(jnp.bfloat16)
    partner = partner_table(pair_order)
    sources = jnp.arange(devices, dtype=jnp.int32)
    partner_dev = 2 * jnp.repeat(partner, 2, axis=1) + sources % 2
    state_parts, gradients = [], []
    for m in range(micro_count):
        partial = jnp.dot(ordered[m], head_weight, preferred_element_type=jnp.float32)
        logits = (partial[:half] + swap(partial[half:], "rep", 1)).astype(jnp.bfloat16)
        tiles = logits.reshape(devices, half // devices, -1)
        tiles = lax.all_to_all(tiles, "rep", split_axis=0, concat_axis=0, tiled=True)
        mates = (partner_dev[m][:, None] == sources[None, :]).astype(jnp.bfloat16)
        mate_tiles = jnp.einsum("ds,srv->drv", mates, tiles, preferred_element_type=jnp.float32)
        graded = difference(tiles, mate_tiles)
        graded = lax.all_to_all(graded, "rep", split_axis=0, concat_axis=0, tiled=True)
        graded = graded.reshape(half, -1)
        gradient = jnp.concatenate([graded, swap(graded, "rep", 1)], axis=0)
        gradients.append(gradient)
        back = jnp.einsum("rv,wv->rw", gradient, head_weight, preferred_element_type=jnp.float32)
        state_canon = sum_over(back, "voc").astype(jnp.bfloat16)
        state_parts.append(
            jnp.einsum("ei,ew->iw", onehot[m], state_canon, preferred_element_type=jnp.float32)
        )
    state_grad = jnp.stack(state_parts).astype(jnp.bfloat16)
    head_grad = jnp.einsum(
        "mrw,mrv->wv", ordered, jnp.stack(gradients), preferred_element_type=jnp.float32
    )
    return state_grad, head_grad.astype(jnp.bfloat16)


def solution(mesh):
    replicas = mesh.shape["rep"] // 2
    few = replicas % 2 == 0 and math.factorial(replicas // 2) <= max_permutations
    few = few and mesh.shape["voc"] == 2
    return jax.shard_map(
        paired_body if few else spread_body,
        mesh=mesh,
        in_specs=(P(None, None, "rep"), P("rep", "voc"), P(), P()),
        out_specs=(P(None, None, "rep"), P("rep", "voc")),
        check_vma=False,
    )
```

```python
import functools
import itertools
import math

import jax
import jax.numpy as jnp
from jax import lax
from jax.experimental import pallas as pl
from jax.experimental.pallas import tpu as pltpu
from jax.sharding import PartitionSpec as P

distill_weight = 0.0625
max_permutations = 24


def partner_table(pair_order):
    slot_count = pair_order.shape[1]
    slot_ids = jnp.arange(slot_count, dtype=jnp.int32)
    matches = pair_order[:, None, :] == slot_ids[None, :, None]
    following = jnp.roll(pair_order, -1, axis=1)
    return jnp.sum(jnp.where(matches, following[:, None, :], 0), axis=2)


def route_kernel(order_ref, *refs):
    *branch_refs, flags_ref, dest, src, color = refs
    micro_count, replicas = order_ref.shape
    pairs = replicas // 2
    replica = lax.axis_index("rep") // 2
    for m in range(micro_count):
        for k in range(replicas):
            to, frm = order_ref[m, k], order_ref[m, (k + 1) % replicas]
            dest[frm] = to
            src[to] = frm
            color[k] = -1
        for start in range(0, replicas, 2):
            at = jnp.where(color[start] == 1, start + 1, start)
            for _ in range(pairs):
                color[at] = 0
                color[at ^ 1] = 1
                at = src[dest[at ^ 1] ^ 1]
        for c in range(2):
            sigma = []
            place = jnp.int32(0)
            for z in range(pairs):
                leaves = jnp.where(color[2 * z] == c, 2 * z, 2 * z + 1)
                to = dest[leaves] // 2
                smaller = to
                for earlier in sigma:
                    smaller = smaller - jnp.where(earlier < to, 1, 0)
                place = place * (pairs - z) + smaller
                sigma.append(to)
            branch_refs[2 * m + c][0] = place
        for row, moved in enumerate((replica, src[replica])):
            at = 2 * m + row
            flags_ref[at : at + 1, :] = jnp.full((1, flags_ref.shape[1]), color[moved], jnp.int32)


def routes(pair_order, width):
    micro_count, replicas = pair_order.shape
    smem = pl.BlockSpec(memory_space=pltpu.SMEM)
    *branches, flags = pl.pallas_call(
        route_kernel,
        out_shape=[jax.ShapeDtypeStruct((1,), jnp.int32)] * (2 * micro_count)
        + [jax.ShapeDtypeStruct((2 * micro_count, width), jnp.int32)],
        in_specs=[smem],
        out_specs=[smem] * (2 * micro_count) + [pl.BlockSpec(memory_space=pltpu.VMEM)],
        scratch_shapes=[pltpu.SMEM((replicas,), jnp.int32)] * 3,
        compiler_params=pltpu.CompilerParams(vmem_limit_bytes=1 << 20),
    )(pair_order)
    branch = [number.reshape(()) for number in branches]
    flag = [flags[at : at + 1] == 0 for at in range(2 * micro_count)]
    return [(branch[2 * m : 2 * m + 2], flag[2 * m : 2 * m + 2]) for m in range(micro_count)]


def move_pairs(block, branch, pairs, beside, *given):
    def one(sigma, moved, *rest):
        if any(z != to for z, to in enumerate(sigma)):
            route = [(z * 4 + low, to * 4 + low) for z, to in enumerate(sigma) for low in range(4)]
            moved = lax.ppermute(moved, "rep", route)
        return moved, beside(*rest)

    every = [functools.partial(one, sigma) for sigma in itertools.permutations(range(pairs))]
    return lax.switch(branch, every, block, *given)


def swap(block, axis, bit):
    count = lax.axis_size(axis)
    return lax.ppermute(block, axis, [(i, i ^ bit) for i in range(count)])


def difference(own, other):
    spread = own.astype(jnp.float32) - other.astype(jnp.float32)
    return (distill_weight * spread).astype(jnp.bfloat16)


def sum_over(block, axis):
    if lax.axis_size(axis) == 2:
        return block + swap(block, axis, 1)
    return lax.psum(block, axis)


def after(block, *others):
    return lax.optimization_barrier((block, *others))[0]


def head_kernel(*refs):
    rows_ref, *blocks, out_ref, whole = refs
    height = blocks[0].shape[0]
    for at, block in enumerate(blocks):
        whole[pl.ds(at * height, height), :] = block[...]
    out_ref[...] = lax.dot_general(
        rows_ref[...], whole[...], (((0,), (0,)), ((), ())), preferred_element_type=jnp.float32
    ).astype(out_ref.dtype)


def head_gradient(rows, blocks):
    count, width = rows.shape
    height, vocab = blocks[0].shape
    step = vocab // 4
    return pl.pallas_call(
        head_kernel,
        grid=(vocab // step,),
        out_shape=jax.ShapeDtypeStruct((width, vocab), jnp.bfloat16),
        in_specs=[pl.BlockSpec((count, width), lambda i: (0, 0))]
        + [pl.BlockSpec((height, step), lambda i: (0, i))] * len(blocks),
        out_specs=pl.BlockSpec((width, step), lambda i: (0, i)),
        scratch_shapes=[pltpu.VMEM((count, step), jnp.bfloat16)],
        compiler_params=pltpu.CompilerParams(vmem_limit_bytes=16 << 20),
        cost_estimate=pl.CostEstimate(
            flops=2 * count * width * vocab,
            bytes_accessed=2 * (count * width + count * vocab + width * vocab),
            transcendentals=0,
        ),
    )(rows, *blocks)


def paired_body(states, head_weight, pair_order, row_example):
    micro_count, row_count, half_width = states.shape
    place = lax.axis_index("rep")
    replica, side = place // 2, place % 2
    parity = replica % 2
    pairs = pair_order.shape[1] // 2
    quarter = row_count // 4
    local = jnp.arange(row_count, dtype=jnp.int32)
    block = local // quarter
    by_core = (block >> 1, block & 1)
    by_chip = (block & 1, block >> 1)
    examples = lax.dynamic_index_in_dim(row_example, replica, 1, keepdims=False)

    def onehots(order):
        other_core, other_chip = order
        example_of = (
            (side ^ other_core) * (2 * quarter) + (parity ^ other_chip) * quarter + local % quarter
        )
        return (examples[:, None, :] == example_of[None, :, None]).astype(jnp.bfloat16)

    onehot_core, onehot_chip = onehots(by_core), onehots(by_chip)

    logits = []
    for m in range(micro_count):
        rows = jnp.dot(onehot_core[m], states[m], preferred_element_type=jnp.float32)
        rows = rows.astype(jnp.bfloat16)
        theirs = jnp.dot(rows[2 * quarter :], head_weight, preferred_element_type=jnp.float32)
        arrived = swap(theirs, "rep", 1)
        own = jnp.dot(rows[: 2 * quarter], head_weight, preferred_element_type=jnp.float32)
        far = (own[quarter:] + arrived[quarter:]).astype(jnp.bfloat16)
        home = (own[:quarter] + arrived[:quarter]).astype(jnp.bfloat16)
        logits.append((home, far))
    sib = swap(logits[0][1], "rep", 2)
    codes = routes(after(pair_order, *logits[-1]), head_weight.shape[1])
    def settle(home, sib, first, second, to_home_first):
        grad_home = difference(home, jnp.where(to_home_first, first, second))
        grad_sib = difference(sib, jnp.where(to_home_first, second, first))
        return grad_home, grad_sib

    def leaving(home, sib, home_first):
        return jnp.where(home_first, home, sib), jnp.where(home_first, sib, home)

    def first_beside(far, waiting):
        return [swap(block, "rep", 2) for block in far], [settle(*group) for group in waiting]

    def second_beside(coming, settled):
        sent = [leaving(*group) for group in coming]
        returned = []
        for grad_home, grad_sib in settled:
            grad_far = swap(grad_sib, "rep", 2)
            near = swap(grad_home, "rep", 1)
            returned.append([grad_home, near, grad_far, swap(grad_far, "rep", 1)])
        return sent, returned

    grads, waiting = [], []
    (branches, (home_first, to_home_first)) = codes[0]
    home = logits[0][0]
    sent = leaving(home, sib, home_first)
    for m in range(micro_count):
        last = m + 1 == micro_count
        first, (arrived, settled) = move_pairs(
            sent[0], branches[0], pairs, first_beside, [] if last else [logits[m + 1][1]], waiting
        )
        coming = [] if last else [(logits[m + 1][0], arrived[0], codes[m + 1][1][0])]
        second, (sents, returned) = move_pairs(
            after(sent[1], first), branches[1], pairs, second_beside, coming, settled
        )
        grads += returned
        waiting = [(home, sib, first, second, to_home_first)]
        if not last:
            (branches, (home_first, to_home_first)) = codes[m + 1]
            home, sib, sent = logits[m + 1][0], arrived[0], sents[0]
    [(grad_home, grad_sib)] = [settle(*group) for group in waiting]
    grad_far = swap(grad_sib, "rep", 2)
    near = swap(grad_home, "rep", 1)
    grads = [[after(block, near) for block in group] for group in grads]
    chip_rows = jnp.einsum(
        "mei,miw->mew", onehot_chip, after(states, near), preferred_element_type=jnp.float32
    )
    chip_rows = chip_rows.astype(jnp.bfloat16)
    grads.append([grad_home, near, grad_far, swap(grad_far, "rep", 1)])

    def back(first, second):
        gradient = jnp.concatenate([first, second], axis=0)
        partial = jnp.einsum(
            "rv,wv->rw", gradient, head_weight, preferred_element_type=jnp.float32
        )
        return partial + swap(partial.astype(jnp.bfloat16), "voc", 1).astype(jnp.float32)

    canon = []
    for group in grads:
        near, far = back(*group[:2]), back(*group[2:])
        canon.append(jnp.concatenate([near, far], axis=0).astype(jnp.bfloat16))
    state_grad = jnp.einsum(
        "mei,mew->miw", onehot_chip, jnp.stack(canon), preferred_element_type=jnp.float32
    ).astype(jnp.bfloat16)
    head_grad = head_gradient(
        chip_rows.reshape(micro_count * row_count, half_width), sum(grads, [])
    )
    return state_grad, head_grad


def spread_body(states, head_weight, pair_order, row_example):
    micro_count, row_count, half_width = states.shape
    devices = lax.axis_size("rep")
    place = lax.axis_index("rep")
    replica, side = place // 2, place % 2
    half = row_count // 2
    local = jnp.arange(row_count, dtype=jnp.int32)
    example_of = (side ^ (local // half)) * half + local % half
    examples = lax.dynamic_index_in_dim(row_example, replica, 1, keepdims=False)
    onehot = (examples[:, None, :] == example_of[None, :, None]).astype(jnp.bfloat16)
    ordered = jnp.einsum("mei,miw->mew", onehot, states, preferred_element_type=jnp.float32)
    ordered = ordered.astype(jnp.bfloat16)
    partner = partner_table(pair_order)
    sources = jnp.arange(devices, dtype=jnp.int32)
    partner_dev = 2 * jnp.repeat(partner, 2, axis=1) + sources % 2
    state_parts, gradients = [], []
    for m in range(micro_count):
        partial = jnp.dot(ordered[m], head_weight, preferred_element_type=jnp.float32)
        logits = (partial[:half] + swap(partial[half:], "rep", 1)).astype(jnp.bfloat16)
        tiles = logits.reshape(devices, half // devices, -1)
        tiles = lax.all_to_all(tiles, "rep", split_axis=0, concat_axis=0, tiled=True)
        mates = (partner_dev[m][:, None] == sources[None, :]).astype(jnp.bfloat16)
        mate_tiles = jnp.einsum("ds,srv->drv", mates, tiles, preferred_element_type=jnp.float32)
        graded = difference(tiles, mate_tiles)
        graded = lax.all_to_all(graded, "rep", split_axis=0, concat_axis=0, tiled=True)
        graded = graded.reshape(half, -1)
        gradient = jnp.concatenate([graded, swap(graded, "rep", 1)], axis=0)
        gradients.append(gradient)
        back = jnp.einsum("rv,wv->rw", gradient, head_weight, preferred_element_type=jnp.float32)
        state_canon = sum_over(back, "voc").astype(jnp.bfloat16)
        state_parts.append(
            jnp.einsum("ei,ew->iw", onehot[m], state_canon, preferred_element_type=jnp.float32)
        )
    state_grad = jnp.stack(state_parts).astype(jnp.bfloat16)
    head_grad = jnp.einsum(
        "mrw,mrv->wv", ordered, jnp.stack(gradients), preferred_element_type=jnp.float32
    )
    return state_grad, head_grad.astype(jnp.bfloat16)


def solution(mesh):
    replicas = mesh.shape["rep"] // 2
    few = replicas % 2 == 0 and math.factorial(replicas // 2) <= max_permutations
    few = few and mesh.shape["voc"] == 2
    return jax.shard_map(
        paired_body if few else spread_body,
        mesh=mesh,
        in_specs=(P(None, None, "rep"), P("rep", "voc"), P(), P()),
        out_specs=(P(None, None, "rep"), P("rep", "voc")),
        check_vma=False,
    )
```

```python
import functools
import itertools
import math

import jax
import jax.numpy as jnp
from jax import lax
from jax.experimental import pallas as pl
from jax.experimental.pallas import tpu as pltpu
from jax.sharding import PartitionSpec as P

distill_weight = 0.0625
max_permutations = 24


def partner_table(pair_order):
    slot_count = pair_order.shape[1]
    slot_ids = jnp.arange(slot_count, dtype=jnp.int32)
    matches = pair_order[:, None, :] == slot_ids[None, :, None]
    following = jnp.roll(pair_order, -1, axis=1)
    return jnp.sum(jnp.where(matches, following[:, None, :], 0), axis=2)


def route_kernel(order_ref, *refs):
    *branch_refs, flags_ref, dest, src, color = refs
    micro_count, replicas = order_ref.shape
    pairs = replicas // 2
    replica = lax.axis_index("rep") // 2
    for m in range(micro_count):
        for k in range(replicas):
            to, frm = order_ref[m, k], order_ref[m, (k + 1) % replicas]
            dest[frm] = to
            src[to] = frm
            color[k] = -1
        for start in range(0, replicas, 2):
            at = jnp.where(color[start] == 1, start + 1, start)
            for _ in range(pairs):
                color[at] = 0
                color[at ^ 1] = 1
                at = src[dest[at ^ 1] ^ 1]
        for c in range(2):
            sigma = []
            place = jnp.int32(0)
            for z in range(pairs):
                leaves = jnp.where(color[2 * z] == c, 2 * z, 2 * z + 1)
                to = dest[leaves] // 2
                smaller = to
                for earlier in sigma:
                    smaller = smaller - jnp.where(earlier < to, 1, 0)
                place = place * (pairs - z) + smaller
                sigma.append(to)
            branch_refs[2 * m + c][0] = place
        for row, moved in enumerate((replica, src[replica])):
            at = 2 * m + row
            flags_ref[at : at + 1, :] = jnp.full((1, flags_ref.shape[1]), color[moved], jnp.int32)


def routes(pair_order, width):
    micro_count, replicas = pair_order.shape
    smem = pl.BlockSpec(memory_space=pltpu.SMEM)
    *branches, flags = pl.pallas_call(
        route_kernel,
        out_shape=[jax.ShapeDtypeStruct((1,), jnp.int32)] * (2 * micro_count)
        + [jax.ShapeDtypeStruct((2 * micro_count, width), jnp.int32)],
        in_specs=[smem],
        out_specs=[smem] * (2 * micro_count) + [pl.BlockSpec(memory_space=pltpu.VMEM)],
        scratch_shapes=[pltpu.SMEM((replicas,), jnp.int32)] * 3,
        compiler_params=pltpu.CompilerParams(vmem_limit_bytes=1 << 20),
    )(pair_order)
    branch = [number.reshape(()) for number in branches]
    flag = [flags[at : at + 1] == 0 for at in range(2 * micro_count)]
    return [(branch[2 * m : 2 * m + 2], flag[2 * m : 2 * m + 2]) for m in range(micro_count)]


def move_pairs(block, branch, pairs, beside, *given):
    def one(sigma, moved, *rest):
        if any(z != to for z, to in enumerate(sigma)):
            route = [(z * 4 + low, to * 4 + low) for z, to in enumerate(sigma) for low in range(4)]
            moved = lax.ppermute(moved, "rep", route)
        return moved, beside(*rest)

    every = [functools.partial(one, sigma) for sigma in itertools.permutations(range(pairs))]
    return lax.switch(branch, every, block, *given)


def swap(block, axis, bit):
    count = lax.axis_size(axis)
    return lax.ppermute(block, axis, [(i, i ^ bit) for i in range(count)])


def difference(own, other):
    spread = own.astype(jnp.float32) - other.astype(jnp.float32)
    return (distill_weight * spread).astype(jnp.bfloat16)


def sum_over(block, axis):
    if lax.axis_size(axis) == 2:
        return block + swap(block, axis, 1)
    return lax.psum(block, axis)


def after(block, *others):
    return lax.optimization_barrier((block, *others))[0]


def head_kernel(*refs):
    rows_ref, *blocks, out_ref, whole = refs
    height = blocks[0].shape[0]
    for at, block in enumerate(blocks):
        whole[pl.ds(at * height, height), :] = block[...]
    out_ref[...] = lax.dot_general(
        rows_ref[...], whole[...], (((0,), (0,)), ((), ())), preferred_element_type=jnp.float32
    ).astype(out_ref.dtype)


def head_gradient(rows, blocks):
    count, width = rows.shape
    height, vocab = blocks[0].shape
    step = vocab // 4
    return pl.pallas_call(
        head_kernel,
        grid=(vocab // step,),
        out_shape=jax.ShapeDtypeStruct((width, vocab), jnp.bfloat16),
        in_specs=[pl.BlockSpec((count, width), lambda i: (0, 0))]
        + [pl.BlockSpec((height, step), lambda i: (0, i))] * len(blocks),
        out_specs=pl.BlockSpec((width, step), lambda i: (0, i)),
        scratch_shapes=[pltpu.VMEM((count, step), jnp.bfloat16)],
        compiler_params=pltpu.CompilerParams(vmem_limit_bytes=16 << 20),
        cost_estimate=pl.CostEstimate(
            flops=2 * count * width * vocab,
            bytes_accessed=2 * (count * width + count * vocab + width * vocab),
            transcendentals=0,
        ),
    )(rows, *blocks)


def paired_body(states, head_weight, pair_order, row_example):
    micro_count, row_count, half_width = states.shape
    place = lax.axis_index("rep")
    replica, side = place // 2, place % 2
    parity = replica % 2
    pairs = pair_order.shape[1] // 2
    quarter = row_count // 4
    local = jnp.arange(row_count, dtype=jnp.int32)
    block = local // quarter
    by_core = (block >> 1, block & 1)
    by_chip = (block & 1, block >> 1)
    examples = lax.dynamic_index_in_dim(row_example, replica, 1, keepdims=False)

    def onehots(order):
        other_core, other_chip = order
        example_of = (
            (side ^ other_core) * (2 * quarter) + (parity ^ other_chip) * quarter + local % quarter
        )
        return (examples[:, None, :] == example_of[None, :, None]).astype(jnp.bfloat16)

    onehot_core, onehot_chip = onehots(by_core), onehots(by_chip)

    logits = []
    for m in range(micro_count):
        rows = jnp.dot(onehot_core[m], states[m], preferred_element_type=jnp.float32)
        rows = rows.astype(jnp.bfloat16)
        theirs = jnp.dot(rows[2 * quarter :], head_weight, preferred_element_type=jnp.float32)
        arrived = swap(theirs, "rep", 1)
        own = jnp.dot(rows[: 2 * quarter], head_weight, preferred_element_type=jnp.float32)
        far = (own[quarter:] + arrived[quarter:]).astype(jnp.bfloat16)
        home = (own[:quarter] + arrived[:quarter]).astype(jnp.bfloat16)
        logits.append((home, far))
    sib = swap(logits[0][1], "rep", 2)
    codes = routes(after(pair_order, *logits[-1]), head_weight.shape[1])
    def settle(home, sib, first, second, to_home_first):
        grad_home = difference(home, jnp.where(to_home_first, first, second))
        grad_sib = difference(sib, jnp.where(to_home_first, second, first))
        return grad_home, grad_sib

    def leaving(home, sib, home_first):
        return jnp.where(home_first, home, sib), jnp.where(home_first, sib, home)

    def beside(nexts, settled):
        arriving = [swap(far, "rep", 2) for far in nexts]
        return arriving, [swap(grad_sib, "rep", 2) for _, grad_sib in settled]

    def second_beside(returned):
        return [(swap(home, "rep", 1), swap(far, "rep", 1)) for home, far in returned]

    early, settled = [], []
    for m in range(micro_count):
        home = logits[m][0]
        branches, (home_first, to_home_first) = codes[m]
        sent = leaving(home, sib, home_first)
        nexts = [] if m + 1 == micro_count else [logits[m + 1][1]]
        if m > 0:
            sent = [after(block, *settled[0]) for block in sent]
        first, (arriving, returned) = move_pairs(
            sent[0], branches[0], pairs, beside, nexts, settled
        )
        returned = [(group[0], far) for group, far in zip(settled, returned)]
        second, swapped = move_pairs(
            after(sent[1], first), branches[1], pairs, second_beside, returned
        )
        for (grad_home, far), (near, farther) in zip(returned, swapped):
            early.append((grad_home, near, far, farther))
        settled = [settle(home, sib, first, second, to_home_first)]
        sib = arriving[0] if arriving else None
    [(grad_home, grad_sib)] = settled
    grads = [list(group) for group in early]
    grad_far = swap(grad_sib, "rep", 2)
    near = swap(grad_home, "rep", 1)
    grads = [[after(block, near) for block in group] for group in grads]
    chip_rows = jnp.einsum(
        "mei,miw->mew", onehot_chip, after(states, near), preferred_element_type=jnp.float32
    )
    chip_rows = chip_rows.astype(jnp.bfloat16)
    grads.append([grad_home, near, grad_far, swap(grad_far, "rep", 1)])

    def back(first, second):
        gradient = jnp.concatenate([first, second], axis=0)
        partial = jnp.einsum(
            "rv,wv->rw", gradient, head_weight, preferred_element_type=jnp.float32
        )
        return partial + swap(partial.astype(jnp.bfloat16), "voc", 1).astype(jnp.float32)

    canon = []
    for group in grads:
        near, far = back(*group[:2]), back(*group[2:])
        canon.append(jnp.concatenate([near, far], axis=0).astype(jnp.bfloat16))
    state_grad = jnp.einsum(
        "mei,mew->miw", onehot_chip, jnp.stack(canon), preferred_element_type=jnp.float32
    ).astype(jnp.bfloat16)
    head_grad = head_gradient(
        chip_rows.reshape(micro_count * row_count, half_width), sum(grads, [])
    )
    return state_grad, head_grad


def spread_body(states, head_weight, pair_order, row_example):
    micro_count, row_count, half_width = states.shape
    devices = lax.axis_size("rep")
    place = lax.axis_index("rep")
    replica, side = place // 2, place % 2
    half = row_count // 2
    local = jnp.arange(row_count, dtype=jnp.int32)
    example_of = (side ^ (local // half)) * half + local % half
    examples = lax.dynamic_index_in_dim(row_example, replica, 1, keepdims=False)
    onehot = (examples[:, None, :] == example_of[None, :, None]).astype(jnp.bfloat16)
    ordered = jnp.einsum("mei,miw->mew", onehot, states, preferred_element_type=jnp.float32)
    ordered = ordered.astype(jnp.bfloat16)
    partner = partner_table(pair_order)
    sources = jnp.arange(devices, dtype=jnp.int32)
    partner_dev = 2 * jnp.repeat(partner, 2, axis=1) + sources % 2
    state_parts, gradients = [], []
    for m in range(micro_count):
        partial = jnp.dot(ordered[m], head_weight, preferred_element_type=jnp.float32)
        logits = (partial[:half] + swap(partial[half:], "rep", 1)).astype(jnp.bfloat16)
        tiles = logits.reshape(devices, half // devices, -1)
        tiles = lax.all_to_all(tiles, "rep", split_axis=0, concat_axis=0, tiled=True)
        mates = (partner_dev[m][:, None] == sources[None, :]).astype(jnp.bfloat16)
        mate_tiles = jnp.einsum("ds,srv->drv", mates, tiles, preferred_element_type=jnp.float32)
        graded = difference(tiles, mate_tiles)
        graded = lax.all_to_all(graded, "rep", split_axis=0, concat_axis=0, tiled=True)
        graded = graded.reshape(half, -1)
        gradient = jnp.concatenate([graded, swap(graded, "rep", 1)], axis=0)
        gradients.append(gradient)
        back = jnp.einsum("rv,wv->rw", gradient, head_weight, preferred_element_type=jnp.float32)
        state_canon = sum_over(back, "voc").astype(jnp.bfloat16)
        state_parts.append(
            jnp.einsum("ei,ew->iw", onehot[m], state_canon, preferred_element_type=jnp.float32)
        )
    state_grad = jnp.stack(state_parts).astype(jnp.bfloat16)
    head_grad = jnp.einsum(
        "mrw,mrv->wv", ordered, jnp.stack(gradients), preferred_element_type=jnp.float32
    )
    return state_grad, head_grad.astype(jnp.bfloat16)


def solution(mesh):
    replicas = mesh.shape["rep"] // 2
    few = replicas % 2 == 0 and math.factorial(replicas // 2) <= max_permutations
    few = few and mesh.shape["voc"] == 2
    return jax.shard_map(
        paired_body if few else spread_body,
        mesh=mesh,
        in_specs=(P(None, None, "rep"), P("rep", "voc"), P(), P()),
        out_specs=(P(None, None, "rep"), P("rep", "voc")),
        check_vma=False,
    )
```

```python
import functools
import itertools
import math

import jax
import jax.numpy as jnp
from jax import lax
from jax.experimental import pallas as pl
from jax.experimental.pallas import tpu as pltpu
from jax.sharding import PartitionSpec as P

distill_weight = 0.0625
max_permutations = 24


def partner_table(pair_order):
    slot_count = pair_order.shape[1]
    slot_ids = jnp.arange(slot_count, dtype=jnp.int32)
    matches = pair_order[:, None, :] == slot_ids[None, :, None]
    following = jnp.roll(pair_order, -1, axis=1)
    return jnp.sum(jnp.where(matches, following[:, None, :], 0), axis=2)


def route_kernel(order_ref, *refs):
    *branch_refs, flags_ref, dest, src, color = refs
    micro_count, replicas = order_ref.shape
    pairs = replicas // 2
    replica = lax.axis_index("rep") // 2
    for m in range(micro_count):
        for k in range(replicas):
            to, frm = order_ref[m, k], order_ref[m, (k + 1) % replicas]
            dest[frm] = to
            src[to] = frm
            color[k] = -1
        for start in range(0, replicas, 2):
            at = jnp.where(color[start] == 1, start + 1, start)
            for _ in range(pairs):
                color[at] = 0
                color[at ^ 1] = 1
                at = src[dest[at ^ 1] ^ 1]
        places, loads = [], []
        for c in range(2):
            sigma = []
            place = jnp.int32(0)
            for z in range(pairs):
                leaves = jnp.where(color[2 * z] == c, 2 * z, 2 * z + 1)
                to = dest[leaves] // 2
                smaller = to
                for earlier in sigma:
                    smaller = smaller - jnp.where(earlier < to, 1, 0)
                place = place * (pairs - z) + smaller
                sigma.append(to)
            load = jnp.int32(0)
            for cut in range(1, pairs):
                over = jnp.int32(0)
                for to in sigma[:cut]:
                    over = over + jnp.where(to >= cut, 1, 0)
                load = jnp.maximum(load, over)
            places.append(place)
            loads.append(load)
        turned = loads[1] > loads[0] if m + 1 < micro_count else loads[1] < loads[0]
        first = jnp.where(turned, 1, 0)
        branch_refs[2 * m][0] = jnp.where(first == 0, places[0], places[1])
        branch_refs[2 * m + 1][0] = jnp.where(first == 0, places[1], places[0])
        for row, moved in enumerate((replica, src[replica])):
            at = 2 * m + row
            flag = jnp.where(color[moved] == first, 0, 1)
            flags_ref[at : at + 1, :] = jnp.full((1, flags_ref.shape[1]), flag, jnp.int32)


def routes(pair_order, width):
    micro_count, replicas = pair_order.shape
    smem = pl.BlockSpec(memory_space=pltpu.SMEM)
    *branches, flags = pl.pallas_call(
        route_kernel,
        out_shape=[jax.ShapeDtypeStruct((1,), jnp.int32)] * (2 * micro_count)
        + [jax.ShapeDtypeStruct((2 * micro_count, width), jnp.int32)],
        in_specs=[smem],
        out_specs=[smem] * (2 * micro_count) + [pl.BlockSpec(memory_space=pltpu.VMEM)],
        scratch_shapes=[pltpu.SMEM((replicas,), jnp.int32)] * 3,
        compiler_params=pltpu.CompilerParams(vmem_limit_bytes=1 << 20),
    )(pair_order)
    branch = [number.reshape(()) for number in branches]
    flag = [flags[at : at + 1] == 0 for at in range(2 * micro_count)]
    return [(branch[2 * m : 2 * m + 2], flag[2 * m : 2 * m + 2]) for m in range(micro_count)]


def move_pairs(block, branch, pairs, beside, *given):
    def one(sigma, moved, *rest):
        if any(z != to for z, to in enumerate(sigma)):
            route = [(z * 4 + low, to * 4 + low) for z, to in enumerate(sigma) for low in range(4)]
            moved = lax.ppermute(moved, "rep", route)
        return moved, beside(*rest)

    every = [functools.partial(one, sigma) for sigma in itertools.permutations(range(pairs))]
    return lax.switch(branch, every, block, *given)


def swap(block, axis, bit):
    count = lax.axis_size(axis)
    return lax.ppermute(block, axis, [(i, i ^ bit) for i in range(count)])


def difference(own, other):
    spread = own.astype(jnp.float32) - other.astype(jnp.float32)
    return (distill_weight * spread).astype(jnp.bfloat16)


def sum_over(block, axis):
    if lax.axis_size(axis) == 2:
        return block + swap(block, axis, 1)
    return lax.psum(block, axis)


def after(block, *others):
    return lax.optimization_barrier((block, *others))[0]


def head_kernel(*refs):
    rows_ref, *blocks, out_ref, whole = refs
    height = blocks[0].shape[0]
    for at, block in enumerate(blocks):
        whole[pl.ds(at * height, height), :] = block[...]
    out_ref[...] = lax.dot_general(
        rows_ref[...], whole[...], (((0,), (0,)), ((), ())), preferred_element_type=jnp.float32
    ).astype(out_ref.dtype)


def head_gradient(rows, blocks):
    count, width = rows.shape
    height, vocab = blocks[0].shape
    step = vocab // 4
    return pl.pallas_call(
        head_kernel,
        grid=(vocab // step,),
        out_shape=jax.ShapeDtypeStruct((width, vocab), jnp.bfloat16),
        in_specs=[pl.BlockSpec((count, width), lambda i: (0, 0))]
        + [pl.BlockSpec((height, step), lambda i: (0, i))] * len(blocks),
        out_specs=pl.BlockSpec((width, step), lambda i: (0, i)),
        scratch_shapes=[pltpu.VMEM((count, step), jnp.bfloat16)],
        compiler_params=pltpu.CompilerParams(vmem_limit_bytes=16 << 20),
        cost_estimate=pl.CostEstimate(
            flops=2 * count * width * vocab,
            bytes_accessed=2 * (count * width + count * vocab + width * vocab),
            transcendentals=0,
        ),
    )(rows, *blocks)


def paired_body(states, head_weight, pair_order, row_example):
    micro_count, row_count, half_width = states.shape
    place = lax.axis_index("rep")
    replica, side = place // 2, place % 2
    parity = replica % 2
    pairs = pair_order.shape[1] // 2
    quarter = row_count // 4
    local = jnp.arange(row_count, dtype=jnp.int32)
    block = local // quarter
    by_core = (block >> 1, block & 1)
    by_chip = (block & 1, block >> 1)
    examples = lax.dynamic_index_in_dim(row_example, replica, 1, keepdims=False)

    def onehots(order):
        other_core, other_chip = order
        example_of = (
            (side ^ other_core) * (2 * quarter) + (parity ^ other_chip) * quarter + local % quarter
        )
        return (examples[:, None, :] == example_of[None, :, None]).astype(jnp.bfloat16)

    onehot_core, onehot_chip = onehots(by_core), onehots(by_chip)

    logits = []
    for m in range(micro_count):
        rows = jnp.dot(onehot_core[m], states[m], preferred_element_type=jnp.float32)
        rows = rows.astype(jnp.bfloat16)
        theirs = jnp.dot(rows[2 * quarter :], head_weight, preferred_element_type=jnp.float32)
        arrived = swap(theirs, "rep", 1)
        own = jnp.dot(rows[: 2 * quarter], head_weight, preferred_element_type=jnp.float32)
        far = (own[quarter:] + arrived[quarter:]).astype(jnp.bfloat16)
        home = (own[:quarter] + arrived[:quarter]).astype(jnp.bfloat16)
        logits.append((home, far))
    sib = swap(logits[0][1], "rep", 2)
    codes = routes(after(pair_order, *logits[-1]), head_weight.shape[1])
    def settle(home, sib, first, second, to_home_first):
        grad_home = difference(home, jnp.where(to_home_first, first, second))
        grad_sib = difference(sib, jnp.where(to_home_first, second, first))
        return grad_home, grad_sib

    def leaving(home, sib, home_first):
        return jnp.where(home_first, home, sib), jnp.where(home_first, sib, home)

    def beside(nexts, settled):
        arriving = [swap(far, "rep", 2) for far in nexts]
        return arriving, [swap(grad_sib, "rep", 2) for _, grad_sib in settled]

    def second_beside(returned):
        return [(swap(home, "rep", 1), swap(far, "rep", 1)) for home, far in returned]

    early, settled = [], []
    for m in range(micro_count):
        home = logits[m][0]
        branches, (home_first, to_home_first) = codes[m]
        sent = leaving(home, sib, home_first)
        nexts = [] if m + 1 == micro_count else [logits[m + 1][1]]
        if m > 0:
            sent = [after(block, *settled[0]) for block in sent]
        first, (arriving, returned) = move_pairs(
            sent[0], branches[0], pairs, beside, nexts, settled
        )
        returned = [(group[0], far) for group, far in zip(settled, returned)]
        second, swapped = move_pairs(
            after(sent[1], first), branches[1], pairs, second_beside, returned
        )
        for (grad_home, far), (near, farther) in zip(returned, swapped):
            early.append((grad_home, near, far, farther))
        settled = [settle(home, sib, first, second, to_home_first)]
        sib = arriving[0] if arriving else None
    [(grad_home, grad_sib)] = settled
    grads = [list(group) for group in early]
    grad_far = swap(grad_sib, "rep", 2)
    near = swap(grad_home, "rep", 1)
    grads = [[after(block, near) for block in group] for group in grads]
    chip_rows = jnp.einsum(
        "mei,miw->mew", onehot_chip, after(states, near), preferred_element_type=jnp.float32
    )
    chip_rows = chip_rows.astype(jnp.bfloat16)
    grads.append([grad_home, near, grad_far, swap(grad_far, "rep", 1)])

    def back(first, second):
        gradient = jnp.concatenate([first, second], axis=0)
        partial = jnp.einsum(
            "rv,wv->rw", gradient, head_weight, preferred_element_type=jnp.float32
        )
        return partial + swap(partial.astype(jnp.bfloat16), "voc", 1).astype(jnp.float32)

    canon = []
    for group in grads:
        near, far = back(*group[:2]), back(*group[2:])
        canon.append(jnp.concatenate([near, far], axis=0).astype(jnp.bfloat16))
    state_grad = jnp.einsum(
        "mei,mew->miw", onehot_chip, jnp.stack(canon), preferred_element_type=jnp.float32
    ).astype(jnp.bfloat16)
    head_grad = head_gradient(
        chip_rows.reshape(micro_count * row_count, half_width), sum(grads, [])
    )
    return state_grad, head_grad


def spread_body(states, head_weight, pair_order, row_example):
    micro_count, row_count, half_width = states.shape
    devices = lax.axis_size("rep")
    place = lax.axis_index("rep")
    replica, side = place // 2, place % 2
    half = row_count // 2
    local = jnp.arange(row_count, dtype=jnp.int32)
    example_of = (side ^ (local // half)) * half + local % half
    examples = lax.dynamic_index_in_dim(row_example, replica, 1, keepdims=False)
    onehot = (examples[:, None, :] == example_of[None, :, None]).astype(jnp.bfloat16)
    ordered = jnp.einsum("mei,miw->mew", onehot, states, preferred_element_type=jnp.float32)
    ordered = ordered.astype(jnp.bfloat16)
    partner = partner_table(pair_order)
    sources = jnp.arange(devices, dtype=jnp.int32)
    partner_dev = 2 * jnp.repeat(partner, 2, axis=1) + sources % 2
    state_parts, gradients = [], []
    for m in range(micro_count):
        partial = jnp.dot(ordered[m], head_weight, preferred_element_type=jnp.float32)
        logits = (partial[:half] + swap(partial[half:], "rep", 1)).astype(jnp.bfloat16)
        tiles = logits.reshape(devices, half // devices, -1)
        tiles = lax.all_to_all(tiles, "rep", split_axis=0, concat_axis=0, tiled=True)
        mates = (partner_dev[m][:, None] == sources[None, :]).astype(jnp.bfloat16)
        mate_tiles = jnp.einsum("ds,srv->drv", mates, tiles, preferred_element_type=jnp.float32)
        graded = difference(tiles, mate_tiles)
        graded = lax.all_to_all(graded, "rep", split_axis=0, concat_axis=0, tiled=True)
        graded = graded.reshape(half, -1)
        gradient = jnp.concatenate([graded, swap(graded, "rep", 1)], axis=0)
        gradients.append(gradient)
        back = jnp.einsum("rv,wv->rw", gradient, head_weight, preferred_element_type=jnp.float32)
        state_canon = sum_over(back, "voc").astype(jnp.bfloat16)
        state_parts.append(
            jnp.einsum("ei,ew->iw", onehot[m], state_canon, preferred_element_type=jnp.float32)
        )
    state_grad = jnp.stack(state_parts).astype(jnp.bfloat16)
    head_grad = jnp.einsum(
        "mrw,mrv->wv", ordered, jnp.stack(gradients), preferred_element_type=jnp.float32
    )
    return state_grad, head_grad.astype(jnp.bfloat16)


def solution(mesh):
    replicas = mesh.shape["rep"] // 2
    few = replicas % 2 == 0 and math.factorial(replicas // 2) <= max_permutations
    few = few and mesh.shape["voc"] == 2
    return jax.shard_map(
        paired_body if few else spread_body,
        mesh=mesh,
        in_specs=(P(None, None, "rep"), P("rep", "voc"), P(), P()),
        out_specs=(P(None, None, "rep"), P("rep", "voc")),
        check_vma=False,
    )
```

```python
import functools
import itertools
import math

import jax
import jax.numpy as jnp
from jax import lax
from jax.experimental import pallas as pl
from jax.experimental.pallas import tpu as pltpu
from jax.sharding import PartitionSpec as P

distill_weight = 0.0625
max_permutations = 24


def partner_table(pair_order):
    slot_count = pair_order.shape[1]
    slot_ids = jnp.arange(slot_count, dtype=jnp.int32)
    matches = pair_order[:, None, :] == slot_ids[None, :, None]
    following = jnp.roll(pair_order, -1, axis=1)
    return jnp.sum(jnp.where(matches, following[:, None, :], 0), axis=2)


def route_kernel(order_ref, *refs):
    *branch_refs, flags_ref, dest, src, color = refs
    micro_count, replicas = order_ref.shape
    pairs = replicas // 2
    replica = lax.axis_index("rep") // 2
    for m in range(micro_count):
        for k in range(replicas):
            to, frm = order_ref[m, k], order_ref[m, (k + 1) % replicas]
            dest[frm] = to
            src[to] = frm
            color[k] = -1
        for start in range(0, replicas, 2):
            at = jnp.where(color[start] == 1, start + 1, start)
            for _ in range(pairs):
                color[at] = 0
                color[at ^ 1] = 1
                at = src[dest[at ^ 1] ^ 1]
        places, loads = [], []
        for c in range(2):
            sigma = []
            place = jnp.int32(0)
            for z in range(pairs):
                leaves = jnp.where(color[2 * z] == c, 2 * z, 2 * z + 1)
                to = dest[leaves] // 2
                smaller = to
                for earlier in sigma:
                    smaller = smaller - jnp.where(earlier < to, 1, 0)
                place = place * (pairs - z) + smaller
                sigma.append(to)
            load = jnp.int32(0)
            for cut in range(1, pairs):
                over = jnp.int32(0)
                for to in sigma[:cut]:
                    over = over + jnp.where(to >= cut, 1, 0)
                load = jnp.maximum(load, over)
            places.append(place)
            loads.append(load)
        turned = loads[1] > loads[0] if m + 1 < micro_count else loads[1] < loads[0]
        first = jnp.where(turned, 1, 0)
        branch_refs[2 * m][0] = jnp.where(first == 0, places[0], places[1])
        branch_refs[2 * m + 1][0] = jnp.where(first == 0, places[1], places[0])
        for row, moved in enumerate((replica, src[replica])):
            at = 2 * m + row
            flag = jnp.where(color[moved] == first, 0, 1)
            flags_ref[at : at + 1, :] = jnp.full((1, flags_ref.shape[1]), flag, jnp.int32)


def routes(pair_order, width):
    micro_count, replicas = pair_order.shape
    smem = pl.BlockSpec(memory_space=pltpu.SMEM)
    *branches, flags = pl.pallas_call(
        route_kernel,
        out_shape=[jax.ShapeDtypeStruct((1,), jnp.int32)] * (2 * micro_count)
        + [jax.ShapeDtypeStruct((2 * micro_count, width), jnp.int32)],
        in_specs=[smem],
        out_specs=[smem] * (2 * micro_count) + [pl.BlockSpec(memory_space=pltpu.VMEM)],
        scratch_shapes=[pltpu.SMEM((replicas,), jnp.int32)] * 3,
        compiler_params=pltpu.CompilerParams(vmem_limit_bytes=1 << 20),
    )(pair_order)
    branch = [number.reshape(()) for number in branches]
    flag = [flags[at : at + 1] == 0 for at in range(2 * micro_count)]
    return [(branch[2 * m : 2 * m + 2], flag[2 * m : 2 * m + 2]) for m in range(micro_count)]


def move_pairs(block, branch, pairs, beside, *given):
    def one(sigma, moved, *rest):
        if any(z != to for z, to in enumerate(sigma)):
            route = [(z * 4 + low, to * 4 + low) for z, to in enumerate(sigma) for low in range(4)]
            moved = lax.ppermute(moved, "rep", route)
        return moved, beside(*rest)

    every = [functools.partial(one, sigma) for sigma in itertools.permutations(range(pairs))]
    return lax.switch(branch, every, block, *given)


def swap(block, axis, bit):
    count = lax.axis_size(axis)
    return lax.ppermute(block, axis, [(i, i ^ bit) for i in range(count)])


def difference(own, other):
    spread = own.astype(jnp.float32) - other.astype(jnp.float32)
    return (distill_weight * spread).astype(jnp.bfloat16)


def sum_over(block, axis):
    if lax.axis_size(axis) == 2:
        return block + swap(block, axis, 1)
    return lax.psum(block, axis)


def after(block, *others):
    return lax.optimization_barrier((block, *others))[0]


def head_kernel(*refs):
    rows_ref, *blocks, out_ref, whole = refs
    height = blocks[0].shape[0]
    for at, block in enumerate(blocks):
        whole[pl.ds(at * height, height), :] = block[...]
    out_ref[...] = lax.dot_general(
        rows_ref[...], whole[...], (((0,), (0,)), ((), ())), preferred_element_type=jnp.float32
    ).astype(out_ref.dtype)


def head_gradient(rows, blocks):
    count, width = rows.shape
    height, vocab = blocks[0].shape
    step = vocab // 4
    return pl.pallas_call(
        head_kernel,
        grid=(vocab // step,),
        out_shape=jax.ShapeDtypeStruct((width, vocab), jnp.bfloat16),
        in_specs=[pl.BlockSpec((count, width), lambda i: (0, 0))]
        + [pl.BlockSpec((height, step), lambda i: (0, i))] * len(blocks),
        out_specs=pl.BlockSpec((width, step), lambda i: (0, i)),
        scratch_shapes=[pltpu.VMEM((count, step), jnp.bfloat16)],
        compiler_params=pltpu.CompilerParams(vmem_limit_bytes=16 << 20),
        cost_estimate=pl.CostEstimate(
            flops=2 * count * width * vocab,
            bytes_accessed=2 * (count * width + count * vocab + width * vocab),
            transcendentals=0,
        ),
    )(rows, *blocks)


def paired_body(states, head_weight, pair_order, row_example):
    micro_count, row_count, half_width = states.shape
    place = lax.axis_index("rep")
    replica, side = place // 2, place % 2
    parity = replica % 2
    pairs = pair_order.shape[1] // 2
    quarter = row_count // 4
    local = jnp.arange(row_count, dtype=jnp.int32)
    block = local // quarter
    by_core = (block >> 1, block & 1)
    by_chip = (block & 1, block >> 1)
    examples = lax.dynamic_index_in_dim(row_example, replica, 1, keepdims=False)

    def onehots(order):
        other_core, other_chip = order
        example_of = (
            (side ^ other_core) * (2 * quarter) + (parity ^ other_chip) * quarter + local % quarter
        )
        return (examples[:, None, :] == example_of[None, :, None]).astype(jnp.bfloat16)

    onehot_core, onehot_chip = onehots(by_core), onehots(by_chip)

    logits = []
    for m in range(micro_count):
        rows = jnp.dot(onehot_core[m], states[m], preferred_element_type=jnp.float32)
        rows = rows.astype(jnp.bfloat16)
        theirs = jnp.dot(rows[2 * quarter :], head_weight, preferred_element_type=jnp.float32)
        arrived = swap(theirs, "rep", 1)
        own = jnp.dot(rows[: 2 * quarter], head_weight, preferred_element_type=jnp.float32)
        far = (own[quarter:] + arrived[quarter:]).astype(jnp.bfloat16)
        home = (own[:quarter] + arrived[:quarter]).astype(jnp.bfloat16)
        logits.append((home, far))
    sib = swap(logits[0][1], "rep", 2)
    codes = routes(after(pair_order, *logits[-1]), head_weight.shape[1])
    def settle(home, sib, first, second, to_home_first):
        grad_home = difference(home, jnp.where(to_home_first, first, second))
        grad_sib = difference(sib, jnp.where(to_home_first, second, first))
        return grad_home, grad_sib

    def leaving(home, sib, home_first):
        return jnp.where(home_first, home, sib), jnp.where(home_first, sib, home)

    def beside(nexts, settled):
        arriving = [swap(far, "rep", 2) for far in nexts]
        return arriving, [swap(grad_sib, "rep", 2) for _, grad_sib in settled]

    def second_beside(returned):
        return [(swap(home, "rep", 1), swap(far, "rep", 1)) for home, far in returned]

    early, settled = [], []
    for m in range(micro_count):
        home = logits[m][0]
        branches, (home_first, to_home_first) = codes[m]
        sent = leaving(home, sib, home_first)
        nexts = [] if m + 1 == micro_count else [logits[m + 1][1]]
        if m > 0:
            sent = [after(block, *settled[0]) for block in sent]
        first, (arriving, returned) = move_pairs(
            sent[0], branches[0], pairs, beside, nexts, settled
        )
        returned = [(group[0], far) for group, far in zip(settled, returned)]
        second, swapped = move_pairs(
            after(sent[1], first), branches[1], pairs, second_beside, returned
        )
        for (grad_home, far), (near, farther) in zip(returned, swapped):
            early.append((grad_home, near, far, farther))
        if m + 1 == micro_count:
            home, sib = leaving(*sent, home_first)
        settled = [settle(home, sib, first, second, to_home_first)]
        sib = arriving[0] if arriving else None
    [(grad_home, grad_sib)] = settled
    grads = [list(group) for group in early]
    grad_far = swap(grad_sib, "rep", 2)
    near = swap(grad_home, "rep", 1)
    grads = [[after(block, near) for block in group] for group in grads]
    chip_rows = jnp.einsum(
        "mei,miw->mew", onehot_chip, after(states, near), preferred_element_type=jnp.float32
    )
    chip_rows = chip_rows.astype(jnp.bfloat16)
    grads.append([grad_home, near, grad_far, swap(grad_far, "rep", 1)])

    def back(first, second):
        gradient = jnp.concatenate([first, second], axis=0)
        partial = jnp.einsum(
            "rv,wv->rw", gradient, head_weight, preferred_element_type=jnp.float32
        )
        return partial + swap(partial.astype(jnp.bfloat16), "voc", 1).astype(jnp.float32)

    canon = []
    for group in grads:
        near, far = back(*group[:2]), back(*group[2:])
        canon.append(jnp.concatenate([near, far], axis=0).astype(jnp.bfloat16))
    state_grad = jnp.einsum(
        "mei,mew->miw", onehot_chip, jnp.stack(canon), preferred_element_type=jnp.float32
    ).astype(jnp.bfloat16)
    head_grad = head_gradient(
        chip_rows.reshape(micro_count * row_count, half_width), sum(grads, [])
    )
    return state_grad, head_grad


def spread_body(states, head_weight, pair_order, row_example):
    micro_count, row_count, half_width = states.shape
    devices = lax.axis_size("rep")
    place = lax.axis_index("rep")
    replica, side = place // 2, place % 2
    half = row_count // 2
    local = jnp.arange(row_count, dtype=jnp.int32)
    example_of = (side ^ (local // half)) * half + local % half
    examples = lax.dynamic_index_in_dim(row_example, replica, 1, keepdims=False)
    onehot = (examples[:, None, :] == example_of[None, :, None]).astype(jnp.bfloat16)
    ordered = jnp.einsum("mei,miw->mew", onehot, states, preferred_element_type=jnp.float32)
    ordered = ordered.astype(jnp.bfloat16)
    partner = partner_table(pair_order)
    sources = jnp.arange(devices, dtype=jnp.int32)
    partner_dev = 2 * jnp.repeat(partner, 2, axis=1) + sources % 2
    state_parts, gradients = [], []
    for m in range(micro_count):
        partial = jnp.dot(ordered[m], head_weight, preferred_element_type=jnp.float32)
        logits = (partial[:half] + swap(partial[half:], "rep", 1)).astype(jnp.bfloat16)
        tiles = logits.reshape(devices, half // devices, -1)
        tiles = lax.all_to_all(tiles, "rep", split_axis=0, concat_axis=0, tiled=True)
        mates = (partner_dev[m][:, None] == sources[None, :]).astype(jnp.bfloat16)
        mate_tiles = jnp.einsum("ds,srv->drv", mates, tiles, preferred_element_type=jnp.float32)
        graded = difference(tiles, mate_tiles)
        graded = lax.all_to_all(graded, "rep", split_axis=0, concat_axis=0, tiled=True)
        graded = graded.reshape(half, -1)
        gradient = jnp.concatenate([graded, swap(graded, "rep", 1)], axis=0)
        gradients.append(gradient)
        back = jnp.einsum("rv,wv->rw", gradient, head_weight, preferred_element_type=jnp.float32)
        state_canon = sum_over(back, "voc").astype(jnp.bfloat16)
        state_parts.append(
            jnp.einsum("ei,ew->iw", onehot[m], state_canon, preferred_element_type=jnp.float32)
        )
    state_grad = jnp.stack(state_parts).astype(jnp.bfloat16)
    head_grad = jnp.einsum(
        "mrw,mrv->wv", ordered, jnp.stack(gradients), preferred_element_type=jnp.float32
    )
    return state_grad, head_grad.astype(jnp.bfloat16)


def solution(mesh):
    replicas = mesh.shape["rep"] // 2
    few = replicas % 2 == 0 and math.factorial(replicas // 2) <= max_permutations
    few = few and mesh.shape["voc"] == 2
    return jax.shard_map(
        paired_body if few else spread_body,
        mesh=mesh,
        in_specs=(P(None, None, "rep"), P("rep", "voc"), P(), P()),
        out_specs=(P(None, None, "rep"), P("rep", "voc")),
        check_vma=False,
    )
```

```python
import functools
import itertools
import math

import jax
import jax.numpy as jnp
from jax import lax
from jax.experimental import pallas as pl
from jax.experimental.pallas import tpu as pltpu
from jax.sharding import PartitionSpec as P

distill_weight = 0.0625
max_permutations = 24


def partner_table(pair_order):
    slot_count = pair_order.shape[1]
    slot_ids = jnp.arange(slot_count, dtype=jnp.int32)
    matches = pair_order[:, None, :] == slot_ids[None, :, None]
    following = jnp.roll(pair_order, -1, axis=1)
    return jnp.sum(jnp.where(matches, following[:, None, :], 0), axis=2)


def route_kernel(order_ref, *refs):
    *branch_refs, flags_ref, dest, src, color = refs
    micro_count, replicas = order_ref.shape
    pairs = replicas // 2
    replica = lax.axis_index("rep") // 2
    for m in range(micro_count):
        for k in range(replicas):
            to, frm = order_ref[m, k], order_ref[m, (k + 1) % replicas]
            dest[frm] = to
            src[to] = frm
            color[k] = -1
        for start in range(0, replicas, 2):
            at = jnp.where(color[start] == 1, start + 1, start)
            for _ in range(pairs):
                color[at] = 0
                color[at ^ 1] = 1
                at = src[dest[at ^ 1] ^ 1]
        places, loads = [], []
        for c in range(2):
            sigma = []
            place = jnp.int32(0)
            for z in range(pairs):
                leaves = jnp.where(color[2 * z] == c, 2 * z, 2 * z + 1)
                to = dest[leaves] // 2
                smaller = to
                for earlier in sigma:
                    smaller = smaller - jnp.where(earlier < to, 1, 0)
                place = place * (pairs - z) + smaller
                sigma.append(to)
            load = jnp.int32(0)
            for cut in range(1, pairs):
                over = jnp.int32(0)
                for to in sigma[:cut]:
                    over = over + jnp.where(to >= cut, 1, 0)
                load = jnp.maximum(load, over)
            places.append(place)
            loads.append(load)
        turned = loads[1] > loads[0] if m + 1 < micro_count else loads[1] < loads[0]
        first = jnp.where(turned, 1, 0)
        branch_refs[2 * m][0] = jnp.where(first == 0, places[0], places[1])
        branch_refs[2 * m + 1][0] = jnp.where(first == 0, places[1], places[0])
        for row, moved in enumerate((replica, src[replica])):
            at = 2 * m + row
            flag = jnp.where(color[moved] == first, 0, 1)
            flags_ref[at : at + 1, :] = jnp.full((1, flags_ref.shape[1]), flag, jnp.int32)


def routes(pair_order, width):
    micro_count, replicas = pair_order.shape
    smem = pl.BlockSpec(memory_space=pltpu.SMEM)
    *branches, flags = pl.pallas_call(
        route_kernel,
        out_shape=[jax.ShapeDtypeStruct((1,), jnp.int32)] * (2 * micro_count)
        + [jax.ShapeDtypeStruct((2 * micro_count, width), jnp.int32)],
        in_specs=[smem],
        out_specs=[smem] * (2 * micro_count) + [pl.BlockSpec(memory_space=pltpu.VMEM)],
        scratch_shapes=[pltpu.SMEM((replicas,), jnp.int32)] * 3,
        compiler_params=pltpu.CompilerParams(vmem_limit_bytes=1 << 20),
    )(pair_order)
    branch = [number.reshape(()) for number in branches]
    flag = [flags[at : at + 1] == 0 for at in range(2 * micro_count)]
    return [(branch[2 * m : 2 * m + 2], flag[2 * m : 2 * m + 2]) for m in range(micro_count)]


def move_pairs(block, branch, pairs, beside, *given):
    def one(sigma, moved, *rest):
        if any(z != to for z, to in enumerate(sigma)):
            route = [(z * 4 + low, to * 4 + low) for z, to in enumerate(sigma) for low in range(4)]
            moved = lax.ppermute(moved, "rep", route)
        return moved, beside(*rest)

    every = [functools.partial(one, sigma) for sigma in itertools.permutations(range(pairs))]
    return lax.switch(branch, every, block, *given)


def swap(block, axis, bit):
    count = lax.axis_size(axis)
    return lax.ppermute(block, axis, [(i, i ^ bit) for i in range(count)])


def difference(own, other):
    spread = own.astype(jnp.float32) - other.astype(jnp.float32)
    return (distill_weight * spread).astype(jnp.bfloat16)


def sum_over(block, axis):
    if lax.axis_size(axis) == 2:
        return block + swap(block, axis, 1)
    return lax.psum(block, axis)


def after(block, *others):
    return lax.optimization_barrier((block, *others))[0]


def head_kernel(*refs):
    rows_ref, *blocks, out_ref, whole = refs
    height = blocks[0].shape[0]
    for at, block in enumerate(blocks):
        whole[pl.ds(at * height, height), :] = block[...]
    out_ref[...] = lax.dot_general(
        rows_ref[...], whole[...], (((0,), (0,)), ((), ())), preferred_element_type=jnp.float32
    ).astype(out_ref.dtype)


def head_gradient(rows, blocks):
    count, width = rows.shape
    height, vocab = blocks[0].shape
    step = vocab // 2
    return pl.pallas_call(
        head_kernel,
        grid=(vocab // step,),
        out_shape=jax.ShapeDtypeStruct((width, vocab), jnp.bfloat16),
        in_specs=[pl.BlockSpec((count, width), lambda i: (0, 0))]
        + [pl.BlockSpec((height, step), lambda i: (0, i))] * len(blocks),
        out_specs=pl.BlockSpec((width, step), lambda i: (0, i)),
        scratch_shapes=[pltpu.VMEM((count, step), jnp.bfloat16)],
        compiler_params=pltpu.CompilerParams(vmem_limit_bytes=16 << 20),
        cost_estimate=pl.CostEstimate(
            flops=2 * count * width * vocab,
            bytes_accessed=2 * (count * width + count * vocab + width * vocab),
            transcendentals=0,
        ),
    )(rows, *blocks)


def paired_body(states, head_weight, pair_order, row_example):
    micro_count, row_count, half_width = states.shape
    place = lax.axis_index("rep")
    replica, side = place // 2, place % 2
    parity = replica % 2
    pairs = pair_order.shape[1] // 2
    quarter = row_count // 4
    local = jnp.arange(row_count, dtype=jnp.int32)
    block = local // quarter
    by_core = (block >> 1, block & 1)
    by_chip = (block & 1, block >> 1)
    examples = lax.dynamic_index_in_dim(row_example, replica, 1, keepdims=False)

    def onehots(order):
        other_core, other_chip = order
        example_of = (
            (side ^ other_core) * (2 * quarter) + (parity ^ other_chip) * quarter + local % quarter
        )
        return (examples[:, None, :] == example_of[None, :, None]).astype(jnp.bfloat16)

    onehot_core, onehot_chip = onehots(by_core), onehots(by_chip)

    logits = []
    for m in range(micro_count):
        rows = jnp.dot(onehot_core[m], states[m], preferred_element_type=jnp.float32)
        rows = rows.astype(jnp.bfloat16)
        theirs = jnp.dot(rows[2 * quarter :], head_weight, preferred_element_type=jnp.float32)
        arrived = swap(theirs, "rep", 1)
        own = jnp.dot(rows[: 2 * quarter], head_weight, preferred_element_type=jnp.float32)
        far = (own[quarter:] + arrived[quarter:]).astype(jnp.bfloat16)
        home = (own[:quarter] + arrived[:quarter]).astype(jnp.bfloat16)
        logits.append((home, far))
    sib = swap(logits[0][1], "rep", 2)
    codes = routes(after(pair_order, *logits[-1]), head_weight.shape[1])
    def settle(home, sib, first, second, to_home_first):
        grad_home = difference(home, jnp.where(to_home_first, first, second))
        grad_sib = difference(sib, jnp.where(to_home_first, second, first))
        return grad_home, grad_sib

    def leaving(home, sib, home_first):
        return jnp.where(home_first, home, sib), jnp.where(home_first, sib, home)

    def beside(nexts, settled):
        arriving = [swap(far, "rep", 2) for far in nexts]
        return arriving, [swap(grad_sib, "rep", 2) for _, grad_sib in settled]

    def second_beside(returned):
        return [(swap(home, "rep", 1), swap(far, "rep", 1)) for home, far in returned]

    early, settled = [], []
    for m in range(micro_count):
        home = logits[m][0]
        branches, (home_first, to_home_first) = codes[m]
        if m > 0:
            home, sib = (after(block, *settled[0]) for block in (home, sib))
        sent = leaving(home, sib, home_first)
        nexts = [] if m + 1 == micro_count else [logits[m + 1][1]]
        first, (arriving, returned) = move_pairs(
            sent[0], branches[0], pairs, beside, nexts, settled
        )
        returned = [(group[0], far) for group, far in zip(settled, returned)]
        second, swapped = move_pairs(
            after(sent[1], first), branches[1], pairs, second_beside, returned
        )
        for (grad_home, far), (near, farther) in zip(returned, swapped):
            early.append((grad_home, near, far, farther))
        if m + 1 == micro_count:
            home, sib = leaving(*sent, home_first)
        settled = [settle(home, sib, first, second, to_home_first)]
        sib = arriving[0] if arriving else None
    [(grad_home, grad_sib)] = settled
    grads = [list(group) for group in early]
    grad_far = swap(grad_sib, "rep", 2)
    near = swap(grad_home, "rep", 1)
    grads = [[after(block, near) for block in group] for group in grads]
    chip_rows = jnp.einsum(
        "mei,miw->mew", onehot_chip, after(states, near), preferred_element_type=jnp.float32
    )
    chip_rows = chip_rows.astype(jnp.bfloat16)
    grads.append([grad_home, near, grad_far, swap(grad_far, "rep", 1)])

    def back(first, second):
        gradient = jnp.concatenate([first, second], axis=0)
        partial = jnp.einsum(
            "rv,wv->rw", gradient, head_weight, preferred_element_type=jnp.float32
        )
        return partial + swap(partial.astype(jnp.bfloat16), "voc", 1).astype(jnp.float32)

    canon = []
    for group in grads:
        near, far = back(*group[:2]), back(*group[2:])
        canon.append(jnp.concatenate([near, far], axis=0).astype(jnp.bfloat16))
    state_grad = jnp.einsum(
        "mei,mew->miw", onehot_chip, jnp.stack(canon), preferred_element_type=jnp.float32
    ).astype(jnp.bfloat16)
    head_grad = head_gradient(
        chip_rows.reshape(micro_count * row_count, half_width), sum(grads, [])
    )
    return state_grad, head_grad


def spread_body(states, head_weight, pair_order, row_example):
    micro_count, row_count, half_width = states.shape
    devices = lax.axis_size("rep")
    place = lax.axis_index("rep")
    replica, side = place // 2, place % 2
    half = row_count // 2
    local = jnp.arange(row_count, dtype=jnp.int32)
    example_of = (side ^ (local // half)) * half + local % half
    examples = lax.dynamic_index_in_dim(row_example, replica, 1, keepdims=False)
    onehot = (examples[:, None, :] == example_of[None, :, None]).astype(jnp.bfloat16)
    ordered = jnp.einsum("mei,miw->mew", onehot, states, preferred_element_type=jnp.float32)
    ordered = ordered.astype(jnp.bfloat16)
    partner = partner_table(pair_order)
    sources = jnp.arange(devices, dtype=jnp.int32)
    partner_dev = 2 * jnp.repeat(partner, 2, axis=1) + sources % 2
    state_parts, gradients = [], []
    for m in range(micro_count):
        partial = jnp.dot(ordered[m], head_weight, preferred_element_type=jnp.float32)
        logits = (partial[:half] + swap(partial[half:], "rep", 1)).astype(jnp.bfloat16)
        tiles = logits.reshape(devices, half // devices, -1)
        tiles = lax.all_to_all(tiles, "rep", split_axis=0, concat_axis=0, tiled=True)
        mates = (partner_dev[m][:, None] == sources[None, :]).astype(jnp.bfloat16)
        mate_tiles = jnp.einsum("ds,srv->drv", mates, tiles, preferred_element_type=jnp.float32)
        graded = difference(tiles, mate_tiles)
        graded = lax.all_to_all(graded, "rep", split_axis=0, concat_axis=0, tiled=True)
        graded = graded.reshape(half, -1)
        gradient = jnp.concatenate([graded, swap(graded, "rep", 1)], axis=0)
        gradients.append(gradient)
        back = jnp.einsum("rv,wv->rw", gradient, head_weight, preferred_element_type=jnp.float32)
        state_canon = sum_over(back, "voc").astype(jnp.bfloat16)
        state_parts.append(
            jnp.einsum("ei,ew->iw", onehot[m], state_canon, preferred_element_type=jnp.float32)
        )
    state_grad = jnp.stack(state_parts).astype(jnp.bfloat16)
    head_grad = jnp.einsum(
        "mrw,mrv->wv", ordered, jnp.stack(gradients), preferred_element_type=jnp.float32
    )
    return state_grad, head_grad.astype(jnp.bfloat16)


def solution(mesh):
    replicas = mesh.shape["rep"] // 2
    few = replicas % 2 == 0 and math.factorial(replicas // 2) <= max_permutations
    few = few and mesh.shape["voc"] == 2
    return jax.shard_map(
        paired_body if few else spread_body,
        mesh=mesh,
        in_specs=(P(None, None, "rep"), P("rep", "voc"), P(), P()),
        out_specs=(P(None, None, "rep"), P("rep", "voc")),
        check_vma=False,
    )
```
